32 devices in a mesh: tile: 4 (over y, x), tm: 8 (over z, core).
Axes of the slice: x: 2, y: 2, z: 4, core: 2. Of those that a mesh axis runs over, the one named last changes fastest.
Arguments:
- movie: bfloat16 [128, 256, 512], P('tm', None, 'tile'), may hold values from -6 to 6
- omega: bfloat16 [2, 4, 32, 128], P(None, 'tile', None, 'tm'), may hold values from -0.5 to 0.5
- time_taps: bfloat16 [17], replicated, may hold values from 0.019897461 to 0.099609375
- space_taps: bfloat16 [17], replicated, may hold values from 0.099609375 to 0.29882812
Outputs:
- basis: float32 [32, 256, 512], P(None, 'tm', 'tile')
- coefficients: float32 [2, 4, 32, 128], P(None, 'tile', None, 'tm')
The draws below stay inside these ranges and needn't reach their ends.
All inputs are finite; a program needn't handle non-finite values.
Results may differ from the reference program's by a relative error of at most 0.024.
Values may be sent and summed in bfloat16 or wider, within the bound.
No kernel may reach another device: no remote copies, remote signals or barrier semaphores. Data moves between devices by JAX's collectives and lax.ppermute only.
A program may use at most 64 MiB of HBM per device.

```python
import math
import jax
import jax.numpy as jnp
from jax import lax

H = 128
W = 128
TY = 2
K = 32
RAD = 8
FR_DEV = 16
FRAMES = 128
ROWS = 256
X = 512
N_TILE = 4
N_TM = 8


def level_of(key, dims, shards, smallest, high):
    level, own = 1.0, jax.random.fold_in(key, 6)
    for dim, blocks in shards:
        draws = jnp.exp(jax.random.uniform(jax.random.fold_in(own, dim), (blocks,), jnp.float32, smallest / len(shards), high / len(shards)))
        level = level * jnp.repeat(draws, dims[dim] // blocks).reshape([-1 if axis == dim else 1 for axis in range(len(dims))])
    return level


def scatter_about(rng, dims, deviation, reach, shards=(), kind=jnp.bfloat16):
    result = jax.random.normal(rng, dims, jnp.float32) * deviation
    if len(shards) > 0:
        result = level_of(rng, dims, shards, -0.22, 0.18) * result
    return jnp.clip(result, min=-reach, max=reach).astype(kind)


def setup_inputs(seed: int = 0) -> dict:
    seeds = jax.random.split(jax.random.key(seed), 5)
    return {
        "movie": scatter_about(seeds[0], (FRAMES, ROWS, X), 1.0, 6.0, ((0, 8), (2, 4))),
        "omega": scatter_about(seeds[1], (TY, N_TILE, K, FRAMES), FRAMES ** -0.5, 0.5, ((1, 4), (3, 8))),
        "time_taps": jnp.clip(jax.random.uniform(seeds[2], (2 * RAD + 1,), jnp.float32, 0.019897461, 0.099609375), 0.019897461, 0.099609375).astype(jnp.bfloat16),
        "space_taps": jnp.clip(jax.random.uniform(seeds[3], (2 * RAD + 1,), jnp.float32, 0.099609375, 0.29882812), 0.099609375, 0.29882812).astype(jnp.bfloat16),
    }


def smooth(field, tap_row, along):
    radius = (tap_row.shape[0] - 1) // 2
    extent = field.shape[along]
    widths = [(0, 0)] * field.ndim
    widths[along] = (radius, radius)
    padded = jnp.pad(field, widths)
    summed = jnp.zeros_like(field)
    for tap_index in range(tap_row.shape[0]):
        summed = summed + tap_row[tap_index] * lax.slice_in_dim(padded, tap_index, tap_index + extent, axis=along)
    return summed

def orthonormal(matrix):
    gram_block = jnp.dot(matrix, matrix.T, precision=lax.Precision.HIGHEST)
    factor_low = jnp.linalg.cholesky(gram_block)
    return jax.scipy.linalg.solve_triangular(factor_low, matrix, lower=True)

def block_sum(left_side, matrix):
    left_blocks = left_side.astype(jnp.float32).reshape(K, N_TM, FR_DEV)
    right_blocks = matrix.astype(jnp.float32).reshape(N_TM, FR_DEV, H * W)
    parts = jnp.einsum('kcf,cfp->ckp', left_blocks, right_blocks)
    return lax.optimization_barrier(jnp.sum(parts.astype(jnp.bfloat16).astype(jnp.float32), axis=0))

def one_tile(pair):
    omega_tile, matrix = pair
    sketch = block_sum(omega_tile, matrix)
    first = orthonormal(sketch).astype(jnp.bfloat16)
    loadings = jnp.dot(matrix.astype(jnp.float32), first.T.astype(jnp.float32), preferred_element_type=jnp.float32).astype(jnp.bfloat16)
    refined = block_sum(loadings.T, matrix)
    final = orthonormal(refined)
    coefficients = lax.dot_general(final.astype(jnp.bfloat16).astype(jnp.float32), matrix.astype(jnp.float32), (((1,), (1,)), ((), ())), preferred_element_type=jnp.float32)
    return ((final * math.sqrt(H * W)).reshape(K, H, W), coefficients)

def reference(movie, omega, time_taps, space_taps):
    time_row = time_taps.astype(jnp.float32)
    space_row = space_taps.astype(jnp.float32)

    def one_column(inputs):
        tile_index, omega_column = inputs
        start = (tile_index * W).astype(jnp.int32)
        centre = lax.dynamic_slice_in_dim(movie, start, W, 2)
        left_rim = lax.dynamic_slice_in_dim(movie, jnp.maximum(start - RAD, 0).astype(jnp.int32), RAD, 2)
        right_rim = lax.dynamic_slice_in_dim(movie, jnp.minimum(start + W, X - RAD).astype(jnp.int32), RAD, 2)
        left_rim = jnp.where(tile_index > 0, left_rim, jnp.zeros_like(left_rim))
        right_rim = jnp.where(tile_index < N_TILE - 1, right_rim, jnp.zeros_like(right_rim))
        extended = jnp.concatenate([left_rim, centre, right_rim], axis=2).astype(jnp.float32)
        temporal = (extended - smooth(extended, time_row, 0)).astype(jnp.bfloat16)
        temporal_f = temporal.astype(jnp.float32)
        smooth_x = jnp.zeros((FRAMES, ROWS, W), jnp.float32)
        for tap_index in range(2 * RAD + 1):
            smooth_x = smooth_x + space_row[tap_index] * temporal_f[:, :, tap_index:tap_index + W]
        smooth_x = smooth_x.astype(jnp.bfloat16).astype(jnp.float32)
        lowpass = smooth(smooth_x, space_row, 1)
        filtered = (temporal_f[:, :, RAD:RAD + W] - lowpass).astype(jnp.bfloat16)
        matrices = jnp.transpose(filtered.reshape(FRAMES, TY, H * W), (1, 0, 2))
        return lax.map(one_tile, (omega_column, matrices))
    bases, coefficients = lax.map(one_column, (jnp.arange(N_TILE, dtype=jnp.int32), jnp.transpose(omega, (1, 0, 2, 3))))
    basis = jnp.transpose(bases, (2, 1, 3, 0, 4)).reshape(K, ROWS, X)
    return (basis, jnp.transpose(coefficients, (1, 0, 2, 3)))
```

```python
import functools
import math

import jax
import jax.numpy as jnp
from jax import lax
from jax.experimental import pallas as pl
from jax.experimental.pallas import tpu as pltpu
from jax.sharding import PartitionSpec as P

TY = 2
VMEM = pl.BlockSpec(memory_space=pltpu.VMEM)
SMEM = pl.BlockSpec(memory_space=pltpu.SMEM)
F32 = jnp.float32
BF16 = jnp.bfloat16
PARAMS = pltpu.CompilerParams(vmem_limit_bytes=40 * 1024 * 1024)


def call(kernel, outs, ins, scratch=(), flops=0):
    moved = sum(v.size * v.dtype.itemsize for v in (*outs, *ins))
    return pl.pallas_call(
        kernel,
        out_shape=outs,
        in_specs=[VMEM] * len(ins),
        out_specs=[VMEM] * len(outs),
        scratch_shapes=scratch,
        compiler_params=PARAMS,
        cost_estimate=pl.CostEstimate(flops=flops, bytes_accessed=moved, transcendentals=0),
    )(*ins)


def toeplitz(taps, rows, cols, shift):
    offsets = (
        lax.broadcasted_iota(jnp.int32, (rows, cols), 1)
        - lax.broadcasted_iota(jnp.int32, (rows, cols), 0)
        + shift
    )
    picks = jnp.arange(taps.shape[0], dtype=jnp.int32)
    hits = (offsets[:, :, None] == picks).astype(F32)
    return jnp.sum(hits * taps.astype(F32), axis=2)


def contract(left, right, left_dim, right_dim):
    return lax.dot_general(
        left, right, (((left_dim,), (right_dim,)), ((), ())), preferred_element_type=F32
    )


def split(value):
    high = value.astype(BF16)
    return high, (value - high.astype(F32)).astype(BF16)


def edges_kernel(x_ref, low_ref, high_ref):
    frames, _, cols = x_ref.shape
    width = low_ref.shape[1]
    row = lax.broadcasted_iota(jnp.int32, (2 * width, cols), 0)
    col = lax.broadcasted_iota(jnp.int32, (2 * width, cols), 1)
    wanted = jnp.where(row < width, row, row + cols - 2 * width)
    pick = jnp.where(col == wanted, 1.0, 0.0).astype(BF16)
    for f in range(frames):
        both = contract(pick, x_ref[f], 1, 1).astype(BF16)
        low_ref[f] = both[:width]
        high_ref[f] = both[width:]


def spatial_kernel(axis, x_ref, hl_ref, hr_ref, bx_ref, bh_ref, dy_ref, om_ref, *rest):
    outs, rows_scr, anchor_scr = rest[:-2], rest[-2], rest[-1]
    frames, rows, cols = x_ref.shape
    count = len(outs)
    share = rows // count
    ranks = om_ref.shape[2]
    me = lax.axis_index(axis)
    bx, bh, dy = bx_ref[...], bh_ref[...], dy_ref[...]

    def halo(f):
        return jnp.concatenate([hl_ref[f].astype(F32), hr_ref[f].astype(F32)], axis=0)

    total = jnp.zeros((rows, cols), F32)
    halo_total = jnp.zeros((bh.shape[0], rows), F32)
    for f in range(frames):
        total = total + x_ref[f].astype(F32)
        halo_total = halo_total + halo(f)
    anchor = (total * (1.0 / frames)).astype(BF16)
    halo_anchor = (halo_total * (1.0 / frames)).astype(BF16)

    def across(block, edge):
        return contract(block, bx, 1, 0) + contract(edge, bh, 0, 0)

    high, low = split(across(anchor, halo_anchor))
    both = contract(dy, jnp.concatenate([high, low], axis=1), 1, 0)
    anchor_s = anchor.astype(F32) - both[:, :cols] - both[:, cols:]
    anchor_out = anchor_s.astype(BF16)
    anchor_scr[...] = anchor_out
    left_over = anchor_s - anchor_out.astype(F32)
    anchor32 = anchor.astype(F32)
    halo32 = halo_anchor.astype(F32)

    def pair(p, carry):
        blocks, smooths = [], []
        for f in (2 * p, 2 * p + 1):
            block = (x_ref[f].astype(F32) - anchor32).astype(BF16)
            edge = (halo(f) - halo32).astype(BF16)
            blocks.append(block)
            smooths.append(across(block, edge).astype(BF16))
        both = contract(dy, jnp.concatenate(smooths, axis=1), 1, 0)
        for i, f in enumerate((2 * p, 2 * p + 1)):
            value = blocks[i].astype(F32) - both[:, i * cols : (i + 1) * cols] + left_over
            rows_scr[pl.ds(f, rows, stride=frames), :] = value
        return carry

    lax.fori_loop(0, frames // 2, pair, 0)
    for k, out in enumerate(outs):
        dest = me ^ k
        start = pl.multiple_of(dest * (share * frames), share * frames)
        block = rows_scr[pl.ds(start, share * frames), :].astype(BF16)
        out[0:share] = block.reshape(share, frames, cols)
        start = pl.multiple_of(dest * share, share)
        out[share : share + share // frames] = anchor_scr[pl.ds(start, share), :].reshape(
            share // frames, frames, cols
        )
        out[share + share // frames, :, 0:ranks] = om_ref[dest // (count // TY)]
        out[share + share // frames, :, ranks:] = jnp.zeros((frames, cols - ranks), BF16)


def temporal_kernel(axis, *refs):
    count = len(refs) - 7
    pieces = refs[:count]
    lhs_ref, m_ref, gram_ref, om_ref, data_scr, anchor_scr, gram_scr = refs[count:]
    share, _, frames, cols = data_scr.shape
    all_frames = count * frames
    me = lax.axis_index(axis)
    for k in range(count):
        src = me ^ k
        data_scr[:, src] = pieces[k][0:share]
        anchor = pieces[k][share : share + share // frames].reshape(share, cols)
        anchor_scr[pl.ds(src, share, stride=count), :] = anchor.astype(F32)
        om_ref[src] = pieces[k][share + share // frames]
    lhs = lhs_ref[...]
    gram_scr[...] = jnp.zeros_like(gram_scr)

    def pair(p, carry):
        blocks, feeds = [], []
        for r in (2 * p, 2 * p + 1):
            block = data_scr[r].reshape(all_frames, cols)
            start = pl.multiple_of(r * count, count)
            anchor = anchor_scr[pl.ds(start, count), :]
            blocks.append(block)
            feeds.append(
                jnp.concatenate([block, jnp.concatenate([anchor, anchor], 0).astype(BF16)], axis=0)
            )
        low = contract(lhs, jnp.concatenate(feeds, axis=1), 1, 0)
        value = (jnp.concatenate(blocks, axis=1).astype(F32) + low).astype(BF16)
        m_ref[2 * p] = value[:, :cols]
        m_ref[2 * p + 1] = value[:, cols:]
        gram_scr[...] += contract(value, value, 1, 1)
        return carry

    lax.fori_loop(0, share // 2, pair, 0)
    gram_ref[...] = gram_scr[...]


def exact(left, right, left_dim, right_dim):
    return lax.dot_general(
        left,
        right,
        (((left_dim,), (right_dim,)), ((), ())),
        precision=lax.Precision.HIGHEST,
        preferred_element_type=F32,
    )


def whiten(gram, *others):
    size = gram.shape[0]
    ids = lax.broadcasted_iota(jnp.int32, (size, 128), 0)
    work = [jnp.concatenate([gram, jnp.zeros((size, 128 - size), F32)], axis=1), *others]
    scale = jnp.zeros((size, 128), F32)
    panel = 8
    for start in range(0, size, panel):
        cols = [
            jnp.broadcast_to(work[0][:, j : j + 1], (size, 128)) for j in range(start, start + panel)
        ]
        for j in range(start, start + panel):
            inverse = 1.0 / cols[j - start][j : j + 1]
            factor = jnp.where(ids > j, cols[j - start] * inverse, 0.0)
            scale = jnp.where(ids == j, inverse, scale)
            for m in range(j - start + 1, panel):
                cols[m] = cols[m] - factor * cols[m][j : j + 1]
            for i in range(len(work)):
                value = work[i]
                width = value.shape[1]
                parts = [
                    value[:, c : c + 128] - factor * value[j : j + 1, c : c + 128]
                    for c in range(0, width, 128)
                ]
                work[i] = parts[0] if len(parts) == 1 else jnp.concatenate(parts, axis=1)
    scale = jnp.sqrt(scale)
    results = []
    for value in work[1:]:
        parts = [value[:, c : c + 128] * scale for c in range(0, value.shape[1], 128)]
        results.append(parts[0] if len(parts) == 1 else jnp.concatenate(parts, axis=1))
    return results


def factor_kernel(axis, count, ranks, pixels, om_ref, *refs):
    grams, (mix_ref, own_ref, send_ref) = refs[:-3], refs[-3:]
    frames = own_ref.shape[1]
    all_frames = grams[0].shape[0]
    me = lax.axis_index(axis)
    gram = grams[0][...]
    for other in grams[1:]:
        gram = gram + other[...]
    omega = om_ref[...].reshape(all_frames, om_ref.shape[2]).astype(F32).T[:ranks]
    sketch = exact(omega, gram, 1, 0)
    (load,) = whiten(exact(sketch, omega, 1, 1), sketch)
    back = exact(load, gram, 1, 0)
    mix, coef = whiten(exact(back, load, 1, 1), load, back)
    mix_ref[...] = mix * math.sqrt(pixels)
    ids = lax.broadcasted_iota(jnp.int32, (all_frames, frames), 0)
    lane = lax.broadcasted_iota(jnp.int32, (all_frames, frames), 1)
    for ref, who in ((own_ref, me), (send_ref, me ^ (count // TY))):
        pick = jnp.where(ids == lane + who * frames, 1.0, 0.0)
        ref[...] = exact(coef, pick, 1, 0)


def basis_kernel(m_ref, mix_ref, out_ref):
    share, _, cols = m_ref.shape
    ranks = mix_ref.shape[0]
    high, low = split(mix_ref[...])
    lhs = jnp.concatenate([high, low], axis=0)
    for p in range(share // 2):
        data = jnp.concatenate([m_ref[2 * p], m_ref[2 * p + 1]], axis=1)
        both = contract(lhs, data, 1, 0)
        value = both[:ranks] + both[ranks:]
        for i in range(2):
            out_ref[pl.ds(2 * p + i, ranks, stride=share), :] = value[:, i * cols : (i + 1) * cols]


def local(movie, omega, time_taps, space_taps):
    frames, rows, cols = movie.shape
    radius = (space_taps.shape[0] - 1) // 2
    count = lax.axis_size("tm")
    tiles = lax.axis_size("tile")
    ranks = omega.shape[2]
    share = rows // count
    all_frames = frames * count
    group = count // TY
    pixels = (rows // TY) * cols

    def shape(dims, dtype):
        return jax.ShapeDtypeStruct(dims, dtype)

    low, high = call(edges_kernel, [shape((frames, radius, rows), BF16)] * 2, [movie])
    right = [(i, i + 1) for i in range(tiles - 1)]
    left = [(j, i) for i, j in right]
    halo_left = lax.ppermute(high, "tile", right)
    halo_right = lax.ppermute(low, "tile", left)

    taps_back = space_taps[::-1]
    bx = toeplitz(taps_back, cols, cols, radius).astype(BF16)
    bh = jnp.concatenate(
        [
            toeplitz(taps_back, radius, cols, 2 * radius),
            toeplitz(taps_back, radius, cols, radius - cols),
        ],
        axis=0,
    ).astype(BF16)
    dy = toeplitz(space_taps, rows, rows, radius).astype(BF16)
    band = toeplitz(time_taps, all_frames, all_frames, radius)
    own = (
        lax.broadcasted_iota(jnp.int32, (all_frames, count), 0) // frames
        == lax.broadcasted_iota(jnp.int32, (all_frames, count), 1)
    ).astype(F32)
    sums = own - jnp.sum(band.reshape(all_frames, count, frames), axis=2)
    sums_high = lax.reduce_precision(sums, 8, 7)
    lhs = jnp.concatenate([-band, sums_high, sums - sums_high], axis=1).astype(BF16)

    om = jnp.transpose(omega[:, 0], (0, 2, 1))
    slots = share + share // frames + 1
    pieces = call(
        functools.partial(spatial_kernel, "tm"),
        [shape((slots, frames, cols), BF16)] * count,
        [movie, halo_left, halo_right, bx, bh, dy, om],
        [pltpu.VMEM((rows * frames, cols), F32), pltpu.VMEM((rows, cols), BF16)],
    )
    pieces = [pieces[0]] + [
        lax.ppermute(pieces[k], "tm", [(i, i ^ k) for i in range(count)]) for k in range(1, count)
    ]
    matrix, gram, om_all = call(
        functools.partial(temporal_kernel, "tm"),
        [
            shape((share, all_frames, cols), BF16),
            shape((all_frames, all_frames), F32),
            shape((count, frames, cols), BF16),
        ],
        [*pieces, lhs],
        [
            pltpu.VMEM((share, count, frames, cols), BF16),
            pltpu.VMEM((share * count, cols), F32),
            pltpu.VMEM((all_frames, all_frames), F32),
        ],
    )
    grams = [gram] + [
        lax.ppermute(gram, "tm", [(i, i ^ k) for i in range(count)]) for k in range(1, group)
    ]
    mix, coef_own, coef_send = call(
        functools.partial(factor_kernel, "tm", count, ranks, pixels),
        [shape((ranks, all_frames), F32), *([shape((ranks, frames), F32)] * 2)],
        [om_all, *grams],
    )
    coef_other = lax.ppermute(coef_send, "tm", [(i, i ^ group) for i in range(count)])
    (basis,) = call(basis_kernel, [shape((ranks * share, cols), F32)], [matrix, mix])
    tile_row = lax.axis_index("tm") // group
    first = jnp.where(tile_row == 0, coef_own, coef_other)
    second = jnp.where(tile_row == 0, coef_other, coef_own)
    return basis.reshape(ranks, share, cols), jnp.stack([first, second])[:, None]


def solution(mesh):
    in_specs = (P("tm", None, "tile"), P(None, "tile", None, "tm"), P(), P())
    out_specs = (P(None, "tm", "tile"), P(None, "tile", None, "tm"))
    return jax.shard_map(local, mesh=mesh, in_specs=in_specs, out_specs=out_specs, check_vma=False)
```

```python
import functools
import math

import jax
import jax.numpy as jnp
from jax import lax
from jax.experimental import pallas as pl
from jax.experimental.pallas import tpu as pltpu
from jax.sharding import PartitionSpec as P

TY = 2
F32 = jnp.float32
BF16 = jnp.bfloat16


def call(kernel, outs, ins, scratch=(), places=None):
    places = places or [pltpu.VMEM] * len(ins)
    return pl.pallas_call(
        kernel,
        out_shape=outs,
        in_specs=[pl.BlockSpec(memory_space=place) for place in places],
        out_specs=[pl.BlockSpec(memory_space=pltpu.VMEM)] * len(outs),
        scratch_shapes=scratch,
        compiler_params=pltpu.CompilerParams(vmem_limit_bytes=40 * 1024 * 1024),
        cost_estimate=pl.CostEstimate(flops=0, bytes_accessed=0, transcendentals=0),
    )(*ins)


def toeplitz(tap_row, rows, cols, shift, sign=1):
    offsets = sign * (
        lax.broadcasted_iota(jnp.int32, (rows, cols), 1)
        - lax.broadcasted_iota(jnp.int32, (rows, cols), 0)
    )
    offsets = offsets + shift
    total = jnp.zeros((rows, cols), F32)
    for t in range(tap_row.shape[1]):
        total = jnp.where(offsets == t, tap_row[:, t : t + 1], total)
    return total


def contract(left, right, left_dim, right_dim):
    return lax.dot_general(
        left, right, (((left_dim,), (right_dim,)), ((), ())), preferred_element_type=F32
    )


def split(value):
    high = value.astype(BF16)
    return high, (value - high.astype(F32)).astype(BF16)


def turned(value, shift):
    return pltpu.roll(value, shift % value.shape[1], 1)


def early_kernel(axis, count, share, x_hbm, taps_ref, *rest):
    head_ref, tail_ref, x_ref, rows_scr, anchor_scr, sem = rest
    frames, rows, cols = x_hbm.shape
    span, part = x_ref.shape[1], 2 * share
    radius = (taps_ref.shape[1] - 1) // 2
    me = lax.axis_index(axis)
    chip = (me // 2) ^ (count // 4)
    first = jnp.clip(chip * part - (span - part) // 2, 0, rows - span)
    first = pl.multiple_of(first, 16)
    inner = pl.multiple_of(chip * part - first, 16)
    copy = pltpu.make_async_copy(x_hbm.at[:, pl.ds(first, span), :], x_ref, sem)
    copy.start()
    taps = taps_ref[...].astype(F32)
    bx = toeplitz(taps, cols, cols, radius, -1).astype(BF16)
    dy = toeplitz(taps, part, span, radius - inner).astype(BF16)
    copy.wait()

    total = jnp.zeros((span, cols), F32)
    for f in range(frames):
        total = total + x_ref[f].astype(F32)
    anchor = (total * (1.0 / frames)).astype(BF16)
    anchor32 = anchor.astype(F32)
    high, low = split(contract(anchor, bx, 1, 0))
    both = contract(dy, jnp.concatenate([high, low], axis=1), 1, 0)
    rows_scr[0:span, :] = anchor32
    centre = rows_scr[pl.ds(inner, part), :]
    anchor_s = centre - both[:, :cols] - both[:, cols:]
    anchor_out = anchor_s.astype(BF16)
    anchor_scr[...] = anchor_out
    left_over = anchor_s - anchor_out.astype(F32)
    for p in range(frames // 2):
        smooths, blocks = [], []
        for f in (2 * p, 2 * p + 1):
            block = (x_ref[f].astype(F32) - anchor32).astype(BF16)
            smooths.append(contract(block, bx, 1, 0).astype(BF16))
            own = x_ref[f, pl.ds(inner, part), :].astype(F32) - centre
            blocks.append(own.astype(BF16).astype(F32))
        both = contract(dy, jnp.concatenate(smooths, axis=1), 1, 0)
        for i, f in enumerate((2 * p, 2 * p + 1)):
            value = blocks[i] - both[:, i * cols : (i + 1) * cols] + left_over
            rows_scr[pl.ds(f, part, stride=frames), :] = value
    lead = head_ref.shape[0] // 2
    rest = share - lead
    for h in range(2):
        index = (me ^ h) % 2
        put_rows(head_ref, h * lead, index * share, lead, rows_scr)
        at = h * (rest + share // frames)
        put_rows(tail_ref, at, index * share + lead, rest, rows_scr)
        put_anchor(tail_ref, at + rest, index * share, share, anchor_scr)


def put_rows(out_ref, at, first, size, rows_scr):
    _, frames, cols = out_ref.shape
    start = pl.multiple_of(first * frames, frames)
    block = rows_scr[pl.ds(start, size * frames), :].astype(BF16)
    out_ref[at : at + size] = block.reshape(size, frames, cols)


def put_anchor(out_ref, at, first, share, anchor_scr):
    _, frames, cols = out_ref.shape
    size = share // frames
    block = anchor_scr[pl.ds(pl.multiple_of(first, share), share), :].astype(BF16)
    out_ref[at : at + size] = block.reshape(size, frames, cols)


def put_edges(out_ref, at, index, rows_scr, anchor_scr, share, frames, width):
    cols = out_ref.shape[2]
    packed = cols // (2 * width)
    groups = share // packed
    lane = lax.broadcasted_iota(jnp.int32, (frames, cols), 1) // (2 * width)
    start = pl.multiple_of(index * (share * frames), share * frames)
    for group in range(groups):
        tile = jnp.zeros((frames, cols), F32)
        for q in range(packed):
            begin = pl.multiple_of(start + (group * packed + q) * frames, frames)
            value = rows_scr[pl.ds(begin, frames), :]
            tile = jnp.where(lane == q, turned(value, width + 2 * width * q), tile)
        out_ref[at + group] = tile.astype(BF16)
    first = pl.multiple_of(index * share, share)
    tile = jnp.zeros((frames, cols), F32)
    for q in range(packed):
        value = jnp.concatenate(
            [
                anchor_scr[pl.ds(first + q, groups, stride=packed), :],
                jnp.zeros((frames - groups, cols), F32),
            ],
            axis=0,
        )
        tile = jnp.where(lane == q, turned(value, width + 2 * width * q), tile)
    out_ref[at + groups] = tile.astype(BF16)


def edges_kernel(x_ref, after_ref, low_ref, high_ref):
    frames, _, cols = x_ref.shape
    width = low_ref.shape[1]
    row = lax.broadcasted_iota(jnp.int32, (2 * width, cols), 0)
    col = lax.broadcasted_iota(jnp.int32, (2 * width, cols), 1)
    wanted = jnp.where(row < width, row, row + cols - 2 * width)
    pick = jnp.where(col == wanted, 1.0, 0.0).astype(BF16)
    for f in range(frames):
        both = contract(pick, x_ref[f], 1, 1).astype(BF16)
        low_ref[f] = both[:width]
        high_ref[f] = both[width:]


def bands_kernel(space_ref, time_ref, bx_ref, bh_ref, dy_ref, lhs_ref):
    rows, cols = dy_ref.shape[0], bx_ref.shape[0]
    space, time = space_ref[...].astype(F32), time_ref[...].astype(F32)
    radius = (space.shape[1] - 1) // 2
    bx_ref[...] = toeplitz(space, cols, cols, radius, -1).astype(BF16)
    bh_ref[0:radius] = toeplitz(space, radius, cols, 0, -1).astype(BF16)
    bh_ref[radius:] = toeplitz(space, radius, cols, radius + cols, -1).astype(BF16)
    dy_ref[...] = toeplitz(space, rows, rows, radius).astype(BF16)
    all_frames = lhs_ref.shape[0]
    count = (lhs_ref.shape[1] - all_frames) // 2
    frames = all_frames // count
    band = toeplitz(time, all_frames, all_frames, radius)
    ids = lax.broadcasted_iota(jnp.int32, (all_frames, count), 0) // frames
    lane = lax.broadcasted_iota(jnp.int32, (all_frames, count), 1)
    sums = jnp.where(ids == lane, 1.0, 0.0)
    for j in range(count):
        piece = jnp.sum(band[:, j * frames : (j + 1) * frames], axis=1, keepdims=True)
        sums = jnp.where(lane == j, sums - piece, sums)
    high, low = split(sums)
    lhs_ref[:, 0:all_frames] = (-band).astype(BF16)
    lhs_ref[:, all_frames:] = jnp.concatenate([high.astype(F32), low.astype(F32)], 1).astype(BF16)


def spatial_kernel(axis, early, x_ref, hl_ref, hr_ref, bx_ref, bh_ref, dy_ref, om_ref, *rest):
    outs, rows_scr, anchor_scr = rest[:-2], rest[-2], rest[-1]
    frames, rows, cols = x_ref.shape
    count = 2 * (len(outs) - 1)
    share = rows // count
    ranks = om_ref.shape[2]
    width = hl_ref.shape[1]
    me = lax.axis_index(axis)
    bx, bh, dy = bx_ref[...], bh_ref[...], dy_ref[...]

    def halo(f):
        return jnp.concatenate([hl_ref[f].astype(F32), hr_ref[f].astype(F32)], axis=0)

    total = jnp.zeros((rows, cols), F32)
    halo_total = jnp.zeros((bh.shape[0], rows), F32)
    for f in range(frames):
        total = total + x_ref[f].astype(F32)
        halo_total = halo_total + halo(f)
    anchor = (total * (1.0 / frames)).astype(BF16)
    halo_anchor = (halo_total * (1.0 / frames)).astype(BF16)

    def across(block, edge):
        return contract(block, bx, 1, 0) + contract(edge, bh, 0, 0)

    high, low = split(across(anchor, halo_anchor))
    both = contract(dy, jnp.concatenate([high, low], axis=1), 1, 0)
    anchor_s = anchor.astype(F32) - both[:, :cols] - both[:, cols:]
    anchor_out = anchor_s.astype(BF16).astype(F32)
    anchor_scr[...] = anchor_out
    left_over = anchor_s - anchor_out
    anchor32 = anchor.astype(F32)
    halo32 = halo_anchor.astype(F32)

    for p in range(frames // 2):
        blocks, smooths = [], []
        for f in (2 * p, 2 * p + 1):
            block = (x_ref[f].astype(F32) - anchor32).astype(BF16)
            edge = (halo(f) - halo32).astype(BF16)
            blocks.append(block)
            smooths.append(across(block, edge).astype(BF16))
        both = contract(dy, jnp.concatenate(smooths, axis=1), 1, 0)
        for i, f in enumerate((2 * p, 2 * p + 1)):
            value = blocks[i].astype(F32) - both[:, i * cols : (i + 1) * cols] + left_over
            rows_scr[pl.ds(f, rows, stride=frames), :] = value

    args = (rows_scr, anchor_scr, share, frames)
    half = share + share // frames
    edge_half = share // (cols // (2 * width)) + 1
    for out, z, blocks in [(outs[0], 0, (0,)), (outs[1], 0, (1,))] + [
        (outs[1 + z // 2], z, (0, 1)) for z in range(2, count, 2)
    ]:
        for i, h in enumerate(blocks):
            dest = me ^ (z + h)
            if z == early:
                put_edges(out, i * edge_half, dest, *args, width)
            else:
                put_rows(out, i * half, dest * share, share, rows_scr)
                put_anchor(out, i * half + share, dest * share, share, anchor_scr)
        last = out.shape[0] - 1
        out[last, :, 0:ranks] = om_ref[(me ^ z) // (count // TY)]
        out[last, :, ranks:] = jnp.zeros((frames, cols - ranks), BF16)


def temporal_kernel(axis, width, early, count, *refs):
    own, pair = refs[:2]
    came, handed = refs[2 : 1 + count // 2], refs[1 + count // 2 : count]
    heads, tails = refs[count : count + 2], refs[count + 2 : count + 4]
    lhs_ref, m_ref, gram_ref, om_ref, data_scr, anchor_scr = refs[count + 4 :]
    share, _, frames, cols = data_scr.shape
    all_frames = count * frames
    me = lax.axis_index(axis)
    packed = cols // (2 * width)
    groups = share // packed
    half = share + share // frames
    lanes = lax.broadcasted_iota(jnp.int32, (frames, cols), 1)
    at_edge = (lanes < width) | (lanes >= cols - width)

    def take_block(ref, at, src):
        data_scr[:, src] = ref[at : at + share]
        anchor = ref[at + share : at + half].reshape(share, cols)
        anchor_scr[pl.ds(src, share, stride=count), :] = anchor.astype(F32)

    def take_edges(head, tail, h, ref, edge_at, src):
        lead = head.shape[0] // 2
        at = h * (half - lead) + share - lead
        anchor = tail[at : at + share // frames].reshape(share, cols).astype(F32)
        anchor_scr[pl.ds(src, share, stride=count), :] = anchor
        last = ref[edge_at + groups].astype(F32)
        for q in range(packed):
            edge = turned(last, -(width + 2 * width * q))[:groups]
            where = pl.ds(src + q * count, groups, stride=count * packed)
            old = anchor_scr[where, :]
            anchor_scr[where, :] = jnp.where(at_edge[:groups], edge, old)
        for group in range(groups):
            tile = ref[edge_at + group].astype(F32)
            for q in range(packed):
                r = group * packed + q
                edge = turned(tile, -(width + 2 * width * q))
                main = head[h * lead + r] if r < lead else tail[h * (half - lead) + r - lead]
                value = jnp.where(at_edge, edge, main.astype(F32))
                data_scr[r, src] = value.astype(BF16)

    for k in range(count):
        src = me ^ k
        z, h = k // 2 * 2, k % 2
        ref = (own, pair)[h] if z == 0 else (came, handed)[h][z // 2 - 1]
        om_ref[src] = ref[ref.shape[0] - 1]
        if z == early:
            take_edges(heads[h], tails[h], h, ref, h * (groups + 1), src)
        else:
            take_block(ref, 0 if z == 0 else h * half, src)
    lhs = lhs_ref[...]
    gram = jnp.zeros((all_frames, all_frames), F32)
    for p in range(share // 2):
        blocks, feeds = [], []
        for r in (2 * p, 2 * p + 1):
            block = data_scr[r].reshape(all_frames, cols)
            anchor = anchor_scr[r * count : (r + 1) * count, :]
            blocks.append(block)
            feeds.append(
                jnp.concatenate([block, jnp.concatenate([anchor, anchor], 0).astype(BF16)], axis=0)
            )
        low = contract(lhs, jnp.concatenate(feeds, axis=1), 1, 0)
        value = (jnp.concatenate(blocks, axis=1).astype(F32) + low).astype(BF16)
        m_ref[2 * p] = value[:, :cols]
        m_ref[2 * p + 1] = value[:, cols:]
        gram = gram + contract(value, value, 1, 1)
    gram_ref[...] = gram


def exact(left, right, left_dim, right_dim):
    return lax.dot_general(
        left,
        right,
        (((left_dim,), (right_dim,)), ((), ())),
        precision=lax.Precision.HIGHEST,
        preferred_element_type=F32,
    )


def whiten(gram, *others):
    size = gram.shape[0]
    ids = lax.broadcasted_iota(jnp.int32, (size, 128), 0)
    work = [jnp.concatenate([gram, jnp.zeros((size, 128 - size), F32)], axis=1), *others]
    scale = jnp.zeros((size, 128), F32)
    panel = 8
    for start in range(0, size, panel):
        cols = [
            jnp.broadcast_to(work[0][:, j : j + 1], (size, 128)) for j in range(start, start + panel)
        ]
        for j in range(start, start + panel):
            inverse = 1.0 / cols[j - start][j : j + 1]
            factor = jnp.where(ids > j, cols[j - start] * inverse, 0.0)
            scale = jnp.where(ids == j, inverse, scale)
            for m in range(j - start + 1, panel):
                cols[m] = cols[m] - factor * cols[m][j : j + 1]
            for i in range(len(work)):
                value = work[i]
                width = value.shape[1]
                parts = [
                    value[:, c : c + 128] - factor * value[j : j + 1, c : c + 128]
                    for c in range(0, width, 128)
                ]
                work[i] = parts[0] if len(parts) == 1 else jnp.concatenate(parts, axis=1)
    scale = jnp.sqrt(scale)
    results = []
    for value in work[1:]:
        parts = [value[:, c : c + 128] * scale for c in range(0, value.shape[1], 128)]
        results.append(parts[0] if len(parts) == 1 else jnp.concatenate(parts, axis=1))
    return results


def factor_kernel(axis, count, ranks, pixels, om_ref, *refs):
    grams, (mix_ref, own_ref, send_ref) = refs[:-3], refs[-3:]
    frames = own_ref.shape[0]
    all_frames = grams[0].shape[0]
    me = lax.axis_index(axis)
    gram = grams[0][...]
    for other in grams[1:]:
        gram = gram + other[...]
    omega = om_ref[...].reshape(all_frames, om_ref.shape[2]).astype(F32).T[:ranks]
    sketch = exact(omega, gram, 1, 0)
    (load,) = whiten(exact(sketch, omega, 1, 1), sketch)
    back = exact(load, gram, 1, 0)
    mix, coef = whiten(exact(back, load, 1, 1), load, back)
    mix_ref[...] = mix * math.sqrt(pixels)
    ids = lax.broadcasted_iota(jnp.int32, (frames, all_frames), 0)
    lane = lax.broadcasted_iota(jnp.int32, (frames, all_frames), 1)
    for ref, who in ((own_ref, me), (send_ref, me ^ (count // TY))):
        pick = jnp.where(lane == ids + who * frames, 1.0, 0.0)
        ref[...] = exact(pick, coef, 1, 1)


def basis_kernel(m_ref, mix_ref, out_ref):
    share, _, cols = m_ref.shape
    ranks = mix_ref.shape[0]
    high, low = split(mix_ref[...])
    lhs = jnp.concatenate([high, low], axis=0)
    for p in range(share // 2):
        data = jnp.concatenate([m_ref[2 * p], m_ref[2 * p + 1]], axis=1)
        both = contract(lhs, data, 1, 0)
        value = both[:ranks] + both[ranks:]
        for i in range(2):
            out_ref[pl.ds(2 * p + i, ranks, stride=share), :] = value[:, i * cols : (i + 1) * cols]


def local(movie, omega, time_taps, space_taps):
    frames, rows, cols = movie.shape
    radius = (space_taps.shape[0] - 1) // 2
    count = lax.axis_size("tm")
    tiles = lax.axis_size("tile")
    ranks = omega.shape[2]
    share = rows // count
    all_frames = frames * count
    group = count // TY
    pixels = (rows // TY) * cols
    early = count // 2
    packed = cols // (2 * radius)
    half = share + share // frames

    def shape(dims, dtype):
        return jax.ShapeDtypeStruct(dims, dtype)

    def swap(value, k):
        return lax.ppermute(value, "tm", [(i, i ^ k) for i in range(count)])

    space_row, time_row = space_taps[None], time_taps[None]
    part = 2 * share
    span = part + 32
    lead = 3 * share // 8
    head, tail = call(
        functools.partial(early_kernel, "tm", count, share),
        [shape((2 * size, frames, cols), BF16) for size in (lead, half - lead)],
        [movie, space_row],
        [
            pltpu.VMEM((frames, span, cols), BF16),
            pltpu.VMEM((part * frames, cols), F32),
            pltpu.VMEM((part, cols), BF16),
            pltpu.SemaphoreType.DMA,
        ],
        [pl.ANY, pltpu.VMEM],
    )
    head_came, tail_came = swap(head, early), swap(tail, early)
    low, high = call(
        edges_kernel,
        [shape((frames, radius, rows), BF16)] * 2,
        [movie, head],
        (),
        [pltpu.VMEM, pl.ANY],
    )
    right = [(i, i + 1) for i in range(tiles - 1)]
    left = [(j, i) for i, j in right]
    halo_left = lax.ppermute(high, "tile", right)
    halo_right = lax.ppermute(low, "tile", left)
    bx, bh, dy, lhs = call(
        bands_kernel,
        [
            shape((cols, cols), BF16),
            shape((2 * radius, cols), BF16),
            shape((rows, rows), BF16),
            shape((all_frames, all_frames + 2 * count), BF16),
        ],
        [space_row, time_row],
    )
    om = jnp.transpose(omega[:, 0], (0, 2, 1))
    slots = [half + 1, half + 1] + [
        2 * (share // packed + 1) + 1 if z == early else 2 * half + 1 for z in range(2, count, 2)
    ]
    own, pair, *parts = call(
        functools.partial(spatial_kernel, "tm", early),
        [shape((n, frames, cols), BF16) for n in slots],
        [movie, halo_left, halo_right, bx, bh, dy, om],
        [pltpu.VMEM((rows * frames, cols), F32), pltpu.VMEM((rows, cols), F32)],
    )
    came = {}

    def send(z, *after):
        value = lax.optimization_barrier((parts[z // 2 - 1], *after))[0]
        came[z] = swap(value, z)

    for z in range(early + 2, count, 2):
        send(z, head_came)
    send(early)
    for z in range(2, early, 2):
        send(z, tail_came, came[early])
    pair = swap(lax.optimization_barrier((pair, came[early]))[0], 1)
    came = [came[z] for z in range(2, count, 2)]
    handed = [swap(value, 1) for value in came]
    mains = [head_came, swap(head_came, 1), tail_came, swap(tail_came, 1)]
    matrix, gram, om_all = call(
        functools.partial(temporal_kernel, "tm", radius, early, count),
        [
            shape((share, all_frames, cols), BF16),
            shape((all_frames, all_frames), F32),
            shape((count, frames, cols), BF16),
        ],
        [own, pair, *came, *handed, *mains, lhs],
        [
            pltpu.VMEM((share, count, frames, cols), BF16),
            pltpu.VMEM((share * count, cols), F32),
        ],
    )
    grams = [gram] + [swap(gram, k) for k in range(1, group)]
    mix, coef_own, coef_send = call(
        functools.partial(factor_kernel, "tm", count, ranks, pixels),
        [shape((ranks, all_frames), F32), *([shape((frames, ranks), F32)] * 2)],
        [om_all, *grams],
    )
    coef_other = swap(coef_send, group)
    (basis,) = call(basis_kernel, [shape((ranks * share, cols), F32)], [matrix, mix])
    tile_row = lax.axis_index("tm") // group
    first = jnp.where(tile_row == 0, coef_own, coef_other)
    second = jnp.where(tile_row == 0, coef_other, coef_own)
    coefficients = jnp.transpose(jnp.stack([first, second]), (0, 2, 1))[:, None]
    return basis.reshape(ranks, share, cols), coefficients


def solution(mesh):
    in_specs = (P("tm", None, "tile"), P(None, "tile", None, "tm"), P(), P())
    out_specs = (P(None, "tm", "tile"), P(None, "tile", None, "tm"))
    return jax.shard_map(local, mesh=mesh, in_specs=in_specs, out_specs=out_specs, check_vma=False)
```

```python
import functools
import math

import jax
import jax.numpy as jnp
from jax import lax
from jax.experimental import pallas as pl
from jax.experimental.pallas import tpu as pltpu
from jax.sharding import PartitionSpec as P

TY = 2
F32 = jnp.float32
BF16 = jnp.bfloat16


def call(kernel, outs, ins, scratch=(), places=None, grant=40 << 20, aliases=None):
    places = places or [pltpu.VMEM] * len(ins)
    return pl.pallas_call(
        kernel,
        out_shape=outs,
        in_specs=[pl.BlockSpec(memory_space=place) for place in places],
        out_specs=[pl.BlockSpec(memory_space=pltpu.VMEM)] * len(outs),
        scratch_shapes=scratch,
        input_output_aliases=aliases or {},
        compiler_params=pltpu.CompilerParams(vmem_limit_bytes=grant),
        cost_estimate=pl.CostEstimate(flops=0, bytes_accessed=0, transcendentals=0),
    )(*ins)


def toeplitz(tap_row, rows, cols, shift, sign=1):
    offsets = sign * (
        lax.broadcasted_iota(jnp.int32, (rows, cols), 1)
        - lax.broadcasted_iota(jnp.int32, (rows, cols), 0)
    )
    offsets = offsets + shift
    total = jnp.zeros((rows, cols), F32)
    for t in range(tap_row.shape[1]):
        total = jnp.where(offsets == t, tap_row[:, t : t + 1], total)
    return total


def contract(left, right, left_dim, right_dim):
    return lax.dot_general(
        left, right, (((left_dim,), (right_dim,)), ((), ())), preferred_element_type=F32
    )


def split(value):
    high = value.astype(BF16)
    return high, (value - high.astype(F32)).astype(BF16)


def turned(value, shift):
    return pltpu.roll(value, shift % value.shape[1], 1)


def device_at(index, count, shift, flip):
    return (index // 2 + shift) % (count // 2) * 2 + (index % 2 + flip) % 2


def put_rows(out_ref, at, first, size, rows_scr):
    _, frames, cols = out_ref.shape
    start = pl.multiple_of(first * frames, frames)
    block = rows_scr[pl.ds(start, size * frames), :].astype(BF16)
    out_ref[at : at + size] = block.reshape(size, frames, cols)


def put_anchor(out_ref, at, first, size, anchor_scr):
    _, frames, cols = out_ref.shape
    block = anchor_scr[pl.ds(pl.multiple_of(first, size), size), :].astype(BF16)
    out_ref[at : at + size // frames] = block.reshape(size // frames, frames, cols)


def put_omega(out_ref, at, omega):
    frames, cols = out_ref.shape[1], out_ref.shape[2]
    ranks = omega.shape[1]
    out_ref[at, :, 0:ranks] = omega
    out_ref[at, :, ranks:] = jnp.zeros((frames, cols - ranks), BF16)


def put_block(out_ref, at, dest, share, rows_scr, anchor_scr):
    put_rows(out_ref, at, dest * share, share, rows_scr)
    put_anchor(out_ref, at + share, dest * share, share, anchor_scr)


def filter_rows(x_of, halo_of, bx, bh, dy, frames, inner, centre_scr, rows_scr, anchor_scr):
    part, span = dy.shape
    cols = bx.shape[0]

    def mean(value_of):
        total = value_of(0)
        for f in range(1, frames):
            total = total + value_of(f)
        return (total * (1.0 / frames)).astype(BF16)

    def across(block, edge):
        value = contract(block, bx, 1, 0)
        return value if edge is None else value + contract(edge, bh, 0, 0)

    def rows_made(value):
        if part == span:
            return value
        centre_scr[...] = value
        return centre_scr[pl.ds(inner, part), :]

    anchor = mean(x_of)
    edge = None if halo_of is None else mean(halo_of)
    anchor32 = anchor.astype(F32)
    edge32 = None if edge is None else edge.astype(F32)
    high, low = split(across(anchor, edge))
    both = contract(dy, jnp.concatenate([high, low], axis=1), 1, 0)
    anchor_s = rows_made(anchor32) - both[:, :cols] - both[:, cols:]
    anchor_out = anchor_s.astype(BF16).astype(F32)
    anchor_scr[...] = anchor_out
    left_over = anchor_s - anchor_out
    for p in range(frames // 2):
        blocks, smooths = [], []
        for f in (2 * p, 2 * p + 1):
            block = (x_of(f) - anchor32).astype(BF16)
            edge = None if halo_of is None else (halo_of(f) - edge32).astype(BF16)
            smooths.append(across(block, edge).astype(BF16))
            blocks.append(rows_made(block.astype(F32)))
        both = contract(dy, jnp.concatenate(smooths, axis=1), 1, 0)
        for i, f in enumerate((2 * p, 2 * p + 1)):
            value = blocks[i] - both[:, i * cols : (i + 1) * cols] + left_over
            rows_scr[pl.ds(f, part, stride=frames), :] = value


def put_edges(out_ref, at, index, rows_scr, anchor_scr, share, frames, width):
    cols = out_ref.shape[2]
    packed = cols // (2 * width)
    groups = share // packed
    lane = lax.broadcasted_iota(jnp.int32, (frames, cols), 1) // (2 * width)
    start = pl.multiple_of(index * (share * frames), share * frames)
    for group in range(groups):
        tile = jnp.zeros((frames, cols), F32)
        for q in range(packed):
            begin = pl.multiple_of(start + (group * packed + q) * frames, frames)
            value = rows_scr[pl.ds(begin, frames), :]
            tile = jnp.where(lane == q, turned(value, width + 2 * width * q), tile)
        out_ref[at + group] = tile.astype(BF16)
    first = pl.multiple_of(index * share, share)
    tile = jnp.zeros((frames, cols), F32)
    for q in range(packed):
        value = jnp.concatenate(
            [
                anchor_scr[pl.ds(first + q, groups, stride=packed), :],
                jnp.zeros((frames - groups, cols), F32),
            ],
            axis=0,
        )
        tile = jnp.where(lane == q, turned(value, width + 2 * width * q), tile)
    out_ref[at + groups] = tile.astype(BF16)


def early_kernel(axis, side, count, x_ref, taps_hbm, *rest):
    out_ref, a_ref, b_ref, *scratch = rest
    taps_ref, centre_scr, rows_scr, anchor_scr, sem = scratch
    frames, rows, cols = x_ref.shape
    part, span = anchor_scr.shape[0], centre_scr.shape[0]
    share = part // 2
    radius = (taps_ref.shape[1] - 1) // 2
    copy = pltpu.make_async_copy(taps_hbm, taps_ref, sem)
    copy.start()
    me = lax.axis_index(axis)
    chip = device_at(me, count, count // 4, 0) // 2
    first = jnp.clip(chip * part - (span - part) // 2, 0, rows - span)
    first = pl.multiple_of(first, 16)
    inner = pl.multiple_of(chip * part - first, 16)
    copy.wait()
    taps = taps_ref[...].astype(F32)
    bx = toeplitz(taps, cols, cols, radius, -1).astype(BF16)
    dy = toeplitz(taps, part, span, radius - inner).astype(BF16)
    scratch = (centre_scr, rows_scr, anchor_scr)

    def x_of(f):
        return x_ref[f, pl.ds(first, span), :].astype(F32)

    filter_rows(x_of, None, bx, None, dy, frames, inner, *scratch)
    for h in range(2):
        put_block(out_ref, h * (share + share // frames), (me + h) % 2, share, rows_scr, anchor_scr)

    row = lax.broadcasted_iota(jnp.int32, (2 * radius, cols), 0)
    col = lax.broadcasted_iota(jnp.int32, (2 * radius, cols), 1)
    right = (row < radius) == (lax.axis_index(side) % 2 == 0)
    wanted = row % radius + jnp.where(right, cols - radius, 0)
    pick = jnp.where(col == wanted, 1.0, 0.0).astype(BF16)
    for f in range(frames):
        both = contract(pick, x_ref[f], 1, 1).astype(BF16)
        a_ref[f] = both[:radius]
        b_ref[f] = both[radius:]


def bands_kernel(side, space_ref, time_ref, bx_ref, bh_ref, dy_ref, lhs_ref):
    rows, cols = dy_ref.shape[0], bx_ref.shape[0]
    space, time = space_ref[...].astype(F32), time_ref[...].astype(F32)
    radius = (space.shape[1] - 1) // 2
    bx_ref[...] = toeplitz(space, cols, cols, radius, -1).astype(BF16)
    left = toeplitz(space, radius, cols, 0, -1)
    right = toeplitz(space, radius, cols, radius + cols, -1)
    odd = lax.axis_index(side) % 2 == 1
    bh_ref[0:radius] = jnp.where(odd, left, right).astype(BF16)
    bh_ref[radius:] = jnp.where(odd, right, left).astype(BF16)
    dy_ref[...] = toeplitz(space, rows, rows, radius).astype(BF16)
    all_frames = lhs_ref.shape[0]
    count = (lhs_ref.shape[1] - all_frames) // 2
    frames = all_frames // count
    band = toeplitz(time, all_frames, all_frames, radius)
    ids = lax.broadcasted_iota(jnp.int32, (all_frames, count), 0) // frames
    lane = lax.broadcasted_iota(jnp.int32, (all_frames, count), 1)
    sums = jnp.where(ids == lane, 1.0, 0.0)
    for j in range(count):
        piece = jnp.sum(band[:, j * frames : (j + 1) * frames], axis=1, keepdims=True)
        sums = jnp.where(lane == j, sums - piece, sums)
    high, low = split(sums)
    lhs_ref[:, 0:all_frames] = (-band).astype(BF16)
    lhs_ref[:, all_frames:] = jnp.concatenate([high.astype(F32), low.astype(F32)], 1).astype(BF16)


def spatial_kernel(axis, x_ref, a_ref, b_ref, bx_ref, bh_ref, dy_ref, om_ref, *rest):
    outs, edge_refs, (rows_scr, anchor_scr) = rest[:-4], rest[-4:-2], rest[-2:]
    frames, rows, cols = x_ref.shape
    radius = a_ref.shape[1]
    share = (outs[0].shape[0] - 1) * frames // (frames + 1)
    count = rows // share
    me = lax.axis_index(axis)

    def halo(f):
        return jnp.concatenate([a_ref[f].astype(F32), b_ref[f].astype(F32)], axis=0)

    scratch = (None, rows_scr, anchor_scr)
    filter_rows(
        lambda f: x_ref[f].astype(F32), halo, bx_ref[...], bh_ref[...], dy_ref[...], frames, 0, *scratch
    )
    early = count // 4
    for (shift, flips), out in zip(message_list(count), outs):
        for i, flip in enumerate(flips):
            dest = device_at(me, count, shift, flip)
            at = i * (share + share // frames + 1)
            put_block(out, at, dest, share, rows_scr, anchor_scr)
            put_omega(out, at + share + share // frames, om_ref[dest // (count // TY)])
    for h, out in enumerate(edge_refs):
        dest = device_at(me, count, early, h)
        put_edges(out, 0, dest, rows_scr, anchor_scr, share, frames, radius)
        put_omega(out, out.shape[0] - 1, om_ref[dest // (count // TY)])


def message_list(count):
    return [(c, (flip,)) for c in range(count // 2) if c != count // 4 for flip in range(2)]


def take_block(data_ref, anchor_ref, ref, at, src):
    share, count, frames, cols = data_ref.shape
    data_ref[:, src] = ref[at : at + share]
    anchor = ref[at + share : at + share + share // frames].reshape(share, cols)
    anchor_ref[pl.ds(src, share, stride=count), :] = anchor.astype(F32)


def take_edges(data_ref, anchor_ref, ref, src, width):
    share, count, frames, cols = data_ref.shape
    packed = cols // (2 * width)
    groups = share // packed
    lanes = lax.broadcasted_iota(jnp.int32, (frames, cols), 1)
    at_edge = (lanes < width) | (lanes >= cols - width)
    last = ref[groups].astype(F32)
    for q in range(packed):
        edge = turned(last, -(width + 2 * width * q))[:groups]
        where = pl.ds(src + q * count, groups, stride=count * packed)
        old = anchor_ref[where, :]
        anchor_ref[where, :] = jnp.where(at_edge[:groups], edge, old)
    for group in range(groups):
        tile = ref[group].astype(F32)
        for q in range(packed):
            r = group * packed + q
            edge = turned(tile, -(width + 2 * width * q))
            value = jnp.where(at_edge, edge, data_ref[r, src].astype(F32))
            data_ref[r, src] = value.astype(BF16)


def gather_kernel(axis, places, *refs):
    blocks, mains, (data_ref, anchor_ref, om_ref) = refs[:-5], refs[-5:-3], refs[-3:]
    share, count, frames, _ = data_ref.shape
    slots = share + share // frames
    me = lax.axis_index(axis)
    for (shift, flip), ref in zip(places, blocks):
        src = device_at(me, count, -shift, flip)
        take_block(data_ref, anchor_ref, ref, 0, src)
        om_ref[src] = ref[slots]
    for h, ref in enumerate(mains):
        take_block(data_ref, anchor_ref, ref, 0, device_at(me, count, -(count // 4), h))


def temporal_kernel(axis, width, places, *refs):
    blocks, edge_refs, lhs_ref = refs[3:-8], refs[-8:-6], refs[-6]
    data_ref, anchor_ref, om_ref, m_ref, gram_ref = refs[-5:]
    share, count, frames, cols = data_ref.shape
    all_frames = count * frames
    slots = share + share // frames
    me = lax.axis_index(axis)
    for (shift, flip), ref in zip(places, blocks):
        src = device_at(me, count, -shift, flip)
        take_block(data_ref, anchor_ref, ref, 0, src)
        om_ref[src] = ref[slots]
    for h, ref in enumerate(edge_refs):
        src = device_at(me, count, -(count // 4), h)
        take_edges(data_ref, anchor_ref, ref, src, width)
        om_ref[src] = ref[ref.shape[0] - 1]
    lhs = lhs_ref[...]
    gram = jnp.zeros((all_frames, all_frames), F32)
    for p in range(share // 2):
        blocks, feeds = [], []
        for r in (2 * p, 2 * p + 1):
            block = data_ref[r].reshape(all_frames, cols)
            anchor = anchor_ref[r * count : (r + 1) * count, :]
            blocks.append(block)
            feeds.append(
                jnp.concatenate([block, jnp.concatenate([anchor, anchor], 0).astype(BF16)], axis=0)
            )
        low = contract(lhs, jnp.concatenate(feeds, axis=1), 1, 0)
        value = (jnp.concatenate(blocks, axis=1).astype(F32) + low).astype(BF16)
        m_ref[2 * p] = value[:, :cols]
        m_ref[2 * p + 1] = value[:, cols:]
        gram = gram + contract(value, value, 1, 1)
    gram_ref[...] = gram


def exact(left, right, left_dim, right_dim):
    return lax.dot_general(
        left,
        right,
        (((left_dim,), (right_dim,)), ((), ())),
        precision=lax.Precision.HIGHEST,
        preferred_element_type=F32,
    )


def whiten(gram, *others):
    size = gram.shape[0]
    ids = lax.broadcasted_iota(jnp.int32, (size, 128), 0)
    work = [jnp.concatenate([gram, jnp.zeros((size, 128 - size), F32)], axis=1), *others]
    scale = jnp.zeros((size, 128), F32)
    panel = 8
    for start in range(0, size, panel):
        cols = [
            jnp.broadcast_to(work[0][:, j : j + 1], (size, 128)) for j in range(start, start + panel)
        ]
        for j in range(start, start + panel):
            inverse = 1.0 / cols[j - start][j : j + 1]
            factor = jnp.where(ids > j, cols[j - start] * inverse, 0.0)
            scale = jnp.where(ids == j, inverse, scale)
            for m in range(j - start + 1, panel):
                cols[m] = cols[m] - factor * cols[m][j : j + 1]
            for i in range(len(work)):
                value = work[i]
                width = value.shape[1]
                parts = [
                    value[:, c : c + 128] - factor * value[j : j + 1, c : c + 128]
                    for c in range(0, width, 128)
                ]
                work[i] = parts[0] if len(parts) == 1 else jnp.concatenate(parts, axis=1)
    scale = jnp.sqrt(scale)
    results = []
    for value in work[1:]:
        parts = [value[:, c : c + 128] * scale for c in range(0, value.shape[1], 128)]
        results.append(parts[0] if len(parts) == 1 else jnp.concatenate(parts, axis=1))
    return results


def factor_kernel(axis, count, ranks, pixels, om_ref, *refs):
    grams, (mix_ref, own_ref, send_ref) = refs[:-3], refs[-3:]
    frames = own_ref.shape[1]
    all_frames = grams[0].shape[0]
    me = lax.axis_index(axis)
    gram = grams[0][...]
    for other in grams[1:]:
        gram = gram + other[...]
    omega = om_ref[...].reshape(all_frames, om_ref.shape[2]).astype(F32).T[:ranks]
    sketch = exact(omega, gram, 1, 0)
    (load,) = whiten(exact(sketch, omega, 1, 1), sketch)
    back = exact(load, gram, 1, 0)
    mix, coef = whiten(exact(back, load, 1, 1), load, back)
    mix_ref[...] = mix * math.sqrt(pixels)
    ids = lax.broadcasted_iota(jnp.int32, (frames, all_frames), 0)
    lane = lax.broadcasted_iota(jnp.int32, (frames, all_frames), 1)
    for ref, who in ((own_ref, me), (send_ref, me ^ (count // TY))):
        pick = jnp.where(lane == ids + who * frames, 1.0, 0.0)
        ref[...] = jnp.zeros_like(ref)
        ref[me // (count // TY)] = exact(pick, coef, 1, 1)


def basis_kernel(m_ref, mix_ref, out_ref):
    share, _, cols = m_ref.shape
    ranks = mix_ref.shape[0]
    high, low = split(mix_ref[...])
    lhs = jnp.concatenate([high, low], axis=0)
    for p in range(share // 2):
        data = jnp.concatenate([m_ref[2 * p], m_ref[2 * p + 1]], axis=1)
        both = contract(lhs, data, 1, 0)
        value = both[:ranks] + both[ranks:]
        for i in range(2):
            out_ref[pl.ds(2 * p + i, ranks, stride=share), :] = value[:, i * cols : (i + 1) * cols]


def local(movie, omega, time_taps, space_taps):
    frames, rows, cols = movie.shape
    radius = (space_taps.shape[0] - 1) // 2
    count = lax.axis_size("tm")
    tiles = lax.axis_size("tile")
    ranks = omega.shape[2]
    share = rows // count
    all_frames = frames * count
    group = count // TY
    pixels = (rows // TY) * cols
    early = count // 4
    packed = cols // (2 * radius)
    slots = share + share // frames

    def shape(dims, dtype):
        return jax.ShapeDtypeStruct(dims, dtype)

    def swap(value, k):
        return lax.ppermute(value, "tm", [(i, i ^ k) for i in range(count)])

    def send(value, shift, flip):
        return lax.ppermute(value, "tm", [(i, device_at(i, count, shift, flip)) for i in range(count)])

    space_row, time_row = space_taps[None], time_taps[None]
    part = 2 * share
    span = part + 32
    main, side_a, side_b = call(
        functools.partial(early_kernel, "tm", "tile", count),
        [
            shape((2 * slots, frames, cols), BF16),
            *([shape((frames, radius, rows), BF16)] * 2),
        ],
        [movie, space_row],
        [
            pltpu.VMEM(space_row.shape, BF16),
            pltpu.VMEM((span, cols), F32),
            pltpu.VMEM((part * frames, cols), F32),
            pltpu.VMEM((part, cols), F32),
            pltpu.SemaphoreType.DMA,
        ],
        [pltpu.VMEM, pltpu.HBM],
    )
    main = send(main, early, 0)
    pairs = [(i, i ^ 1) for i in range(tiles)]
    side_a = lax.ppermute(side_a, "tile", pairs)
    pairs = [(i, i + 1) for i in range(1, tiles - 1, 2)]
    side_b = lax.ppermute(side_b, "tile", pairs + [(j, i) for i, j in pairs])
    bx, bh, dy, lhs = call(
        functools.partial(bands_kernel, "tile"),
        [
            shape((cols, cols), BF16),
            shape((2 * radius, cols), BF16),
            shape((rows, rows), BF16),
            shape((all_frames, all_frames + 2 * count), BF16),
        ],
        [space_row, time_row],
    )
    om = jnp.transpose(omega[:, 0], (0, 2, 1))
    listed = message_list(count)
    *parts, edges, edges_other = call(
        functools.partial(spatial_kernel, "tm"),
        [
            *[shape((len(flips) * (slots + 1), frames, cols), BF16) for _, flips in listed],
            *([shape((share // packed + 2, frames, cols), BF16)] * 2),
        ],
        [movie, side_a, side_b, bx, bh, dy, om],
        [pltpu.VMEM((rows * frames, cols), F32), pltpu.VMEM((rows, cols), F32)],
    )
    edges, edges_other = send(edges, early, 0), send(edges_other, early, 1)
    came = [
        send(value, shift, flips[0] if len(flips) == 1 else 0)
        for (shift, flips), value in zip(listed[2:], parts[2:])
    ]
    blocks = [parts[0], send(parts[1], 0, 1)]
    for (_, flips), value in zip(listed[2:], came):
        blocks += [value] if len(flips) == 1 else [value, swap(value[slots + 1 :], 1)]
    places = [(shift, flip) for shift, flips in listed for flip in flips]
    known = call(
        functools.partial(gather_kernel, "tm", places[:-2]),
        [
            shape((share, count, frames, cols), BF16),
            shape((share * count, cols), F32),
            shape((count, frames, cols), BF16),
        ],
        [*blocks[:-2], main, swap(main[slots:], 1)],
    )
    _, _, om_all, matrix, gram = call(
        functools.partial(temporal_kernel, "tm", radius, places[-2:]),
        [
            *[shape(value.shape, value.dtype) for value in known],
            shape((share, all_frames, cols), BF16),
            shape((all_frames, all_frames), F32),
        ],
        [*known, *blocks[-2:], edges, edges_other, lhs],
        aliases={0: 0, 1: 1, 2: 2},
    )
    grams = [gram] + [swap(gram, k) for k in range(1, group)]
    mix, coef_own, coef_send = call(
        functools.partial(factor_kernel, "tm", count, ranks, pixels),
        [shape((ranks, all_frames), F32), *([shape((TY, frames, ranks), F32)] * 2)],
        [om_all, *grams],
    )
    coef_other = swap(coef_send, group)
    (basis,) = call(basis_kernel, [shape((ranks * share, cols), F32)], [matrix, mix])
    coefficients = jnp.transpose(coef_own + coef_other, (0, 2, 1))[:, None]
    return basis.reshape(ranks, share, cols), coefficients


def solution(mesh):
    in_specs = (P("tm", None, "tile"), P(None, "tile", None, "tm"), P(), P())
    out_specs = (P(None, "tm", "tile"), P(None, "tile", None, "tm"))
    return jax.shard_map(local, mesh=mesh, in_specs=in_specs, out_specs=out_specs, check_vma=False)
```

```python
import functools
import math

import jax
import jax.numpy as jnp
from jax import lax
from jax.experimental import pallas as pl
from jax.experimental.pallas import tpu as pltpu
from jax.sharding import PartitionSpec as P

TY = 2
F32 = jnp.float32
BF16 = jnp.bfloat16


def call(kernel, outs, ins, scratch=(), places=None, grant=40 << 20, aliases=None):
    places = places or [pltpu.VMEM] * len(ins)
    return pl.pallas_call(
        kernel,
        out_shape=outs,
        in_specs=[pl.BlockSpec(memory_space=place) for place in places],
        out_specs=[pl.BlockSpec(memory_space=pltpu.VMEM)] * len(outs),
        scratch_shapes=scratch,
        input_output_aliases=aliases or {},
        compiler_params=pltpu.CompilerParams(vmem_limit_bytes=grant),
        cost_estimate=pl.CostEstimate(flops=0, bytes_accessed=0, transcendentals=0),
    )(*ins)


def toeplitz(tap_row, rows, cols, shift, sign=1):
    offsets = sign * (
        lax.broadcasted_iota(jnp.int32, (rows, cols), 1)
        - lax.broadcasted_iota(jnp.int32, (rows, cols), 0)
    )
    offsets = offsets + shift
    total = jnp.zeros((rows, cols), F32)
    for t in range(tap_row.shape[1]):
        total = jnp.where(offsets == t, tap_row[:, t : t + 1], total)
    return total


def contract(left, right, left_dim, right_dim):
    return lax.dot_general(
        left, right, (((left_dim,), (right_dim,)), ((), ())), preferred_element_type=F32
    )


def split(value):
    high = value.astype(BF16)
    return high, (value - high.astype(F32)).astype(BF16)


def turned(value, shift):
    return pltpu.roll(value, shift % value.shape[1], 1)


def device_at(index, count, shift, flip):
    return (index // 2 + shift) % (count // 2) * 2 + (index % 2 + flip) % 2


def put_rows(out_ref, at, first, size, rows_scr):
    _, frames, cols = out_ref.shape
    start = pl.multiple_of(first * frames, frames)
    block = rows_scr[pl.ds(start, size * frames), :].astype(BF16)
    out_ref[at : at + size] = block.reshape(size, frames, cols)


def put_anchor(out_ref, at, first, size, anchor_scr):
    _, frames, cols = out_ref.shape
    block = anchor_scr[pl.ds(pl.multiple_of(first, size), size), :].astype(BF16)
    out_ref[at : at + size // frames] = block.reshape(size // frames, frames, cols)


def put_omega(out_ref, at, omega):
    frames, cols = out_ref.shape[1], out_ref.shape[2]
    ranks = omega.shape[1]
    out_ref[at, :, 0:ranks] = omega
    out_ref[at, :, ranks:] = jnp.zeros((frames, cols - ranks), BF16)


def put_block(out_ref, at, dest, share, rows_scr, anchor_scr):
    put_rows(out_ref, at, dest * share, share, rows_scr)
    put_anchor(out_ref, at + share, dest * share, share, anchor_scr)


def filter_rows(x_of, halo_of, bx, bh, dy, frames, inner, centre_scr, rows_scr, anchor_scr):
    part, span = dy.shape
    cols = bx.shape[0]

    def mean(value_of):
        total = value_of(0)
        for f in range(1, frames):
            total = total + value_of(f)
        return (total * (1.0 / frames)).astype(BF16)

    def across(block, edge):
        value = contract(block, bx, 1, 0)
        return value if edge is None else value + contract(edge, bh, 0, 0)

    def rows_made(value):
        if part == span:
            return value
        centre_scr[...] = value
        return centre_scr[pl.ds(inner, part), :]

    anchor = mean(x_of)
    edge = None if halo_of is None else mean(halo_of)
    anchor32 = anchor.astype(F32)
    edge32 = None if edge is None else edge.astype(F32)
    high, low = split(across(anchor, edge))
    both = contract(dy, jnp.concatenate([high, low], axis=1), 1, 0)
    anchor_s = rows_made(anchor32) - both[:, :cols] - both[:, cols:]
    anchor_out = anchor_s.astype(BF16).astype(F32)
    anchor_scr[...] = anchor_out
    left_over = anchor_s - anchor_out
    for p in range(frames // 2):
        blocks, smooths = [], []
        for f in (2 * p, 2 * p + 1):
            block = (x_of(f) - anchor32).astype(BF16)
            edge = None if halo_of is None else (halo_of(f) - edge32).astype(BF16)
            smooths.append(across(block, edge).astype(BF16))
            blocks.append(rows_made(block.astype(F32)))
        both = contract(dy, jnp.concatenate(smooths, axis=1), 1, 0)
        for i, f in enumerate((2 * p, 2 * p + 1)):
            value = blocks[i] - both[:, i * cols : (i + 1) * cols] + left_over
            rows_scr[pl.ds(f, part, stride=frames), :] = value


def put_edges(out_ref, at, index, rows_scr, anchor_scr, share, frames, width):
    cols = out_ref.shape[2]
    packed = cols // (2 * width)
    groups = share // packed
    lane = lax.broadcasted_iota(jnp.int32, (frames, cols), 1) // (2 * width)
    start = pl.multiple_of(index * (share * frames), share * frames)
    for group in range(groups):
        tile = jnp.zeros((frames, cols), F32)
        for q in range(packed):
            begin = pl.multiple_of(start + (group * packed + q) * frames, frames)
            value = rows_scr[pl.ds(begin, frames), :]
            tile = jnp.where(lane == q, turned(value, width + 2 * width * q), tile)
        out_ref[at + group] = tile.astype(BF16)
    first = pl.multiple_of(index * share, share)
    tile = jnp.zeros((frames, cols), F32)
    for q in range(packed):
        value = jnp.concatenate(
            [
                anchor_scr[pl.ds(first + q, groups, stride=packed), :],
                jnp.zeros((frames - groups, cols), F32),
            ],
            axis=0,
        )
        tile = jnp.where(lane == q, turned(value, width + 2 * width * q), tile)
    out_ref[at + groups] = tile.astype(BF16)


def early_kernel(axis, side, count, x_ref, taps_hbm, *rest):
    outs, (a_ref, b_ref), scratch = rest[:2], rest[2:4], rest[4:]
    taps_ref, centre_scr, rows_scr, anchor_scr, sem = scratch
    frames, rows, cols = x_ref.shape
    part, span = anchor_scr.shape[0], centre_scr.shape[0]
    share = part // 2
    radius = (taps_ref.shape[1] - 1) // 2
    copy = pltpu.make_async_copy(taps_hbm, taps_ref, sem)
    copy.start()
    me = lax.axis_index(axis)
    chip = device_at(me, count, count // 4, 0) // 2
    first = jnp.clip(chip * part - (span - part) // 2, 0, rows - span)
    first = pl.multiple_of(first, 16)
    inner = pl.multiple_of(chip * part - first, 16)
    copy.wait()
    taps = taps_ref[...].astype(F32)
    bx = toeplitz(taps, cols, cols, radius, -1).astype(BF16)
    dy = toeplitz(taps, part, span, radius - inner).astype(BF16)
    scratch = (centre_scr, rows_scr, anchor_scr)

    def x_of(f):
        return x_ref[f, pl.ds(first, span), :].astype(F32)

    filter_rows(x_of, None, bx, None, dy, frames, inner, *scratch)
    for h, out_ref in enumerate(outs):
        put_block(out_ref, 0, (me + h) % 2, share, rows_scr, anchor_scr)

    row = lax.broadcasted_iota(jnp.int32, (2 * radius, cols), 0)
    col = lax.broadcasted_iota(jnp.int32, (2 * radius, cols), 1)
    right = (row < radius) == (lax.axis_index(side) % 2 == 0)
    wanted = row % radius + jnp.where(right, cols - radius, 0)
    pick = jnp.where(col == wanted, 1.0, 0.0).astype(BF16)
    for f in range(frames):
        both = contract(pick, x_ref[f], 1, 1).astype(BF16)
        a_ref[f] = both[:radius]
        b_ref[f] = both[radius:]


def prepare_kernel(side, x_ref, space_ref, time_ref, om_in, bh_ref, dy_ref, lhs_ref, om_ref, *rest):
    anchor_ref, block_ref, smooth_ref = rest
    om_ref[...] = om_in[...]
    frames, rows, cols = x_ref.shape
    space, time = space_ref[...].astype(F32), time_ref[...].astype(F32)
    radius = (space.shape[1] - 1) // 2
    bx = toeplitz(space, cols, cols, radius, -1).astype(BF16)
    total = jnp.zeros((rows, cols), F32)
    for f in range(frames):
        total = total + x_ref[f].astype(F32)
    anchor = (total * (1.0 / frames)).astype(BF16)
    anchor32 = anchor.astype(F32)
    anchor_ref[...] = anchor32
    smooth_ref[frames] = contract(anchor, bx, 1, 0)
    for f in range(frames):
        block = (x_ref[f].astype(F32) - anchor32).astype(BF16)
        block_ref[f] = block
        smooth_ref[f] = contract(block, bx, 1, 0)
    left = toeplitz(space, radius, cols, 0, -1)
    right = toeplitz(space, radius, cols, radius + cols, -1)
    odd = lax.axis_index(side) % 2 == 1
    bh_ref[0:radius] = jnp.where(odd, left, right).astype(BF16)
    bh_ref[radius:] = jnp.where(odd, right, left).astype(BF16)
    dy_ref[...] = toeplitz(space, rows, rows, radius).astype(BF16)
    all_frames = lhs_ref.shape[0]
    count = (lhs_ref.shape[1] - all_frames) // 2
    frames = all_frames // count
    band = toeplitz(time, all_frames, all_frames, radius)
    ids = lax.broadcasted_iota(jnp.int32, (all_frames, count), 0) // frames
    lane = lax.broadcasted_iota(jnp.int32, (all_frames, count), 1)
    sums = jnp.where(ids == lane, 1.0, 0.0)
    for j in range(count):
        piece = jnp.sum(band[:, j * frames : (j + 1) * frames], axis=1, keepdims=True)
        sums = jnp.where(lane == j, sums - piece, sums)
    high, low = split(sums)
    lhs_ref[:, 0:all_frames] = (-band).astype(BF16)
    lhs_ref[:, all_frames:] = jnp.concatenate([high.astype(F32), low.astype(F32)], 1).astype(BF16)


def spatial_kernel(axis, a_ref, b_ref, bh_ref, dy_ref, om_ref, *rest):
    (anchor_ref, block_ref, smooth_ref), rest = rest[:3], rest[3:]
    outs, edge_refs, (rows_scr, anchor_scr) = rest[:-4], rest[-4:-2], rest[-2:]
    frames, rows, cols = block_ref.shape
    radius = a_ref.shape[1]
    share = (outs[0].shape[0] - 1) * frames // (frames + 1)
    count = rows // share
    me = lax.axis_index(axis)
    bh, dy = bh_ref[...], dy_ref[...]

    def halo(f):
        return jnp.concatenate([a_ref[f].astype(F32), b_ref[f].astype(F32)], axis=0)

    def across(f, edge):
        return smooth_ref[f] + contract(edge, bh, 0, 0)

    total = halo(0)
    for f in range(1, frames):
        total = total + halo(f)
    edge_anchor = (total * (1.0 / frames)).astype(BF16)
    edge32 = edge_anchor.astype(F32)
    high, low = split(across(frames, edge_anchor))
    both = contract(dy, jnp.concatenate([high, low], axis=1), 1, 0)
    anchor_s = anchor_ref[...] - both[:, :cols] - both[:, cols:]
    anchor_out = anchor_s.astype(BF16).astype(F32)
    anchor_scr[...] = anchor_out
    left_over = anchor_s - anchor_out
    for p in range(frames // 2):
        pair = (2 * p, 2 * p + 1)
        smooths = [across(f, (halo(f) - edge32).astype(BF16)).astype(BF16) for f in pair]
        both = contract(dy, jnp.concatenate(smooths, axis=1), 1, 0)
        for i, f in enumerate(pair):
            value = block_ref[f].astype(F32) - both[:, i * cols : (i + 1) * cols] + left_over
            rows_scr[pl.ds(f, rows, stride=frames), :] = value
    early = count // 4
    for (shift, flips), out in zip(message_list(count), outs):
        for i, flip in enumerate(flips):
            dest = device_at(me, count, shift, flip)
            at = i * (share + share // frames + 1)
            put_block(out, at, dest, share, rows_scr, anchor_scr)
            put_omega(out, at + share + share // frames, om_ref[dest // (count // TY)])
    for h, out in enumerate(edge_refs):
        dest = device_at(me, count, early, h)
        put_edges(out, 0, dest, rows_scr, anchor_scr, share, frames, radius)
        put_omega(out, out.shape[0] - 1, om_ref[dest // (count // TY)])


def message_list(count):
    return [(c, (flip,)) for c in range(count // 2) if c != count // 4 for flip in range(2)]


def take_block(data_ref, anchor_ref, ref, at, src):
    share, count, frames, cols = data_ref.shape
    data_ref[:, src] = ref[at : at + share]
    anchor = ref[at + share : at + share + share // frames].reshape(share, cols)
    anchor_ref[pl.ds(src, share, stride=count), :] = anchor.astype(F32)


def take_edges(data_ref, anchor_ref, ref, src, width):
    share, count, frames, cols = data_ref.shape
    packed = cols // (2 * width)
    groups = share // packed
    lanes = lax.broadcasted_iota(jnp.int32, (frames, cols), 1)
    at_edge = (lanes < width) | (lanes >= cols - width)
    last = ref[groups].astype(F32)
    for q in range(packed):
        edge = turned(last, -(width + 2 * width * q))[:groups]
        where = pl.ds(src + q * count, groups, stride=count * packed)
        old = anchor_ref[where, :]
        anchor_ref[where, :] = jnp.where(at_edge[:groups], edge, old)
    for group in range(groups):
        tile = ref[group].astype(F32)
        for q in range(packed):
            r = group * packed + q
            edge = turned(tile, -(width + 2 * width * q))
            value = jnp.where(at_edge, edge, data_ref[r, src].astype(F32))
            data_ref[r, src] = value.astype(BF16)


def gather_kernel(axis, places, *refs):
    blocks, mains, (data_ref, anchor_ref, om_ref) = refs[:-5], refs[-5:-3], refs[-3:]
    share, count, frames, _ = data_ref.shape
    slots = share + share // frames
    me = lax.axis_index(axis)
    for (shift, flip), ref in zip(places, blocks):
        src = device_at(me, count, -shift, flip)
        take_block(data_ref, anchor_ref, ref, 0, src)
        om_ref[src] = ref[slots]
    for h, ref in enumerate(mains):
        take_block(data_ref, anchor_ref, ref, 0, device_at(me, count, -(count // 4), h))


def temporal_kernel(axis, width, places, *refs):
    blocks, edge_refs, lhs_ref = refs[3:-8], refs[-8:-6], refs[-6]
    data_ref, anchor_ref, om_ref, m_ref, gram_ref = refs[-5:]
    share, count, frames, cols = data_ref.shape
    all_frames = count * frames
    slots = share + share // frames
    me = lax.axis_index(axis)
    for (shift, flip), ref in zip(places, blocks):
        src = device_at(me, count, -shift, flip)
        take_block(data_ref, anchor_ref, ref, 0, src)
        om_ref[src] = ref[slots]
    for h, ref in enumerate(edge_refs):
        src = device_at(me, count, -(count // 4), h)
        take_edges(data_ref, anchor_ref, ref, src, width)
        om_ref[src] = ref[ref.shape[0] - 1]
    lhs = lhs_ref[...]
    gram = jnp.zeros((all_frames, all_frames), F32)
    for p in range(share // 2):
        blocks, feeds = [], []
        for r in (2 * p, 2 * p + 1):
            block = data_ref[r].reshape(all_frames, cols)
            anchor = anchor_ref[r * count : (r + 1) * count, :]
            blocks.append(block)
            feeds.append(
                jnp.concatenate([block, jnp.concatenate([anchor, anchor], 0).astype(BF16)], axis=0)
            )
        low = contract(lhs, jnp.concatenate(feeds, axis=1), 1, 0)
        value = (jnp.concatenate(blocks, axis=1).astype(F32) + low).astype(BF16)
        m_ref[2 * p] = value[:, :cols]
        m_ref[2 * p + 1] = value[:, cols:]
        gram = gram + contract(value, value, 1, 1)
    gram_ref[...] = gram


def exact(left, right, left_dim, right_dim):
    return lax.dot_general(
        left,
        right,
        (((left_dim,), (right_dim,)), ((), ())),
        precision=lax.Precision.HIGHEST,
        preferred_element_type=F32,
    )


def whiten(gram, *others):
    size = gram.shape[0]
    ids = lax.broadcasted_iota(jnp.int32, (size, 128), 0)
    work = [jnp.concatenate([gram, jnp.zeros((size, 128 - size), F32)], axis=1), *others]
    scale = jnp.zeros((size, 128), F32)
    panel = 16
    for start in range(0, size, panel):
        cols = [
            jnp.broadcast_to(work[0][:, j : j + 1], (size, 128)) for j in range(start, start + panel)
        ]
        for j in range(start, start + panel):
            inverse = 1.0 / cols[j - start][j : j + 1]
            factor = jnp.where(ids > j, cols[j - start] * inverse, 0.0)
            scale = jnp.where(ids == j, inverse, scale)
            for m in range(j - start + 1, panel):
                cols[m] = cols[m] - factor * cols[m][j : j + 1]
            for i in range(len(work)):
                value = work[i]
                width = value.shape[1]
                parts = [
                    value[:, c : c + 128] - factor * value[j : j + 1, c : c + 128]
                    for c in range(0, width, 128)
                ]
                work[i] = parts[0] if len(parts) == 1 else jnp.concatenate(parts, axis=1)
    scale = jnp.sqrt(scale)
    results = []
    for value in work[1:]:
        parts = [value[:, c : c + 128] * scale for c in range(0, value.shape[1], 128)]
        results.append(parts[0] if len(parts) == 1 else jnp.concatenate(parts, axis=1))
    return results


def factor_kernel(axis, count, ranks, pixels, om_ref, *refs):
    grams, (mix_ref, own_ref, send_ref) = refs[:-3], refs[-3:]
    frames = own_ref.shape[1]
    all_frames = grams[0].shape[0]
    me = lax.axis_index(axis)
    gram = grams[0][...]
    for other in grams[1:]:
        gram = gram + other[...]
    omega = om_ref[...].reshape(all_frames, om_ref.shape[2]).astype(F32).T[:ranks]
    sketch = exact(omega, gram, 1, 0)
    (load,) = whiten(exact(sketch, omega, 1, 1), sketch)
    back = exact(load, gram, 1, 0)
    mix, coef = whiten(exact(back, load, 1, 1), load, back)
    mix_ref[...] = mix * math.sqrt(pixels)
    ids = lax.broadcasted_iota(jnp.int32, (frames, all_frames), 0)
    lane = lax.broadcasted_iota(jnp.int32, (frames, all_frames), 1)
    for ref, who in ((own_ref, me), (send_ref, me ^ (count // TY))):
        pick = jnp.where(lane == ids + who * frames, 1.0, 0.0)
        ref[...] = jnp.zeros_like(ref)
        ref[me // (count // TY)] = exact(pick, coef, 1, 1)


def basis_kernel(m_ref, mix_ref, out_ref):
    share, _, cols = m_ref.shape
    ranks = mix_ref.shape[0]
    high, low = split(mix_ref[...])
    lhs = jnp.concatenate([high, low], axis=0)
    for p in range(share // 2):
        data = jnp.concatenate([m_ref[2 * p], m_ref[2 * p + 1]], axis=1)
        both = contract(lhs, data, 1, 0)
        value = both[:ranks] + both[ranks:]
        for i in range(2):
            out_ref[pl.ds(2 * p + i, ranks, stride=share), :] = value[:, i * cols : (i + 1) * cols]


def local(movie, omega, time_taps, space_taps):
    frames, rows, cols = movie.shape
    radius = (space_taps.shape[0] - 1) // 2
    count = lax.axis_size("tm")
    tiles = lax.axis_size("tile")
    ranks = omega.shape[2]
    share = rows // count
    all_frames = frames * count
    group = count // TY
    pixels = (rows // TY) * cols
    early = count // 4
    packed = cols // (2 * radius)
    slots = share + share // frames

    def shape(dims, dtype):
        return jax.ShapeDtypeStruct(dims, dtype)

    def swap(value, k):
        return lax.ppermute(value, "tm", [(i, i ^ k) for i in range(count)])

    def send(value, shift, flip):
        return lax.ppermute(value, "tm", [(i, device_at(i, count, shift, flip)) for i in range(count)])

    space_row, time_row = space_taps[None], time_taps[None]
    part = 2 * share
    span = part + 32
    *mains, side_a, side_b = call(
        functools.partial(early_kernel, "tm", "tile", count),
        [
            *([shape((slots, frames, cols), BF16)] * 2),
            *([shape((frames, radius, rows), BF16)] * 2),
        ],
        [movie, space_row],
        [
            pltpu.VMEM(space_row.shape, BF16),
            pltpu.VMEM((span, cols), F32),
            pltpu.VMEM((part * frames, cols), F32),
            pltpu.VMEM((part, cols), F32),
            pltpu.SemaphoreType.DMA,
        ],
        [pltpu.VMEM, pltpu.HBM],
    )
    mains = [send(value, early, h) for h, value in enumerate(mains)]
    pairs = [(i, i ^ 1) for i in range(tiles)]
    side_a = lax.ppermute(side_a, "tile", pairs)
    pairs = [(i, i + 1) for i in range(1, tiles - 1, 2)]
    side_b = lax.ppermute(side_b, "tile", pairs + [(j, i) for i, j in pairs])
    om = jnp.transpose(omega[:, 0], (0, 2, 1))
    bh, dy, lhs, om, *prepared = call(
        functools.partial(prepare_kernel, "tile"),
        [
            shape((2 * radius, cols), BF16),
            shape((rows, rows), BF16),
            shape((all_frames, all_frames + 2 * count), BF16),
            shape(om.shape, om.dtype),
            shape((rows, cols), F32),
            shape(movie.shape, BF16),
            shape((frames + 1, rows, cols), F32),
        ],
        [movie, space_row, time_row, om],
    )
    listed = message_list(count)
    *parts, edges, edges_other = call(
        functools.partial(spatial_kernel, "tm"),
        [
            *[shape((len(flips) * (slots + 1), frames, cols), BF16) for _, flips in listed],
            *([shape((share // packed + 2, frames, cols), BF16)] * 2),
        ],
        [side_a, side_b, bh, dy, om, *prepared],
        [pltpu.VMEM((rows * frames, cols), F32), pltpu.VMEM((rows, cols), F32)],
    )
    def after(value, other):
        return lax.optimization_barrier((value, other))[0]

    parts[-2:] = [after(value, other) for value, other in zip(parts[-2:], mains)]
    blocks = [parts[0]] + [
        send(value, shift, flip) for (shift, (flip,)), value in zip(listed[1:], parts[1:])
    ]
    edges = send(after(edges, blocks[1]), early, 0)
    edges_other = send(after(edges_other, blocks[1]), early, 1)
    places = [(shift, flip) for shift, flips in listed for flip in flips]
    known = call(
        functools.partial(gather_kernel, "tm", places[:-2]),
        [
            shape((share, count, frames, cols), BF16),
            shape((share * count, cols), F32),
            shape((count, frames, cols), BF16),
        ],
        [*blocks[:-2], *mains],
    )
    _, _, om_all, matrix, gram = call(
        functools.partial(temporal_kernel, "tm", radius, places[-2:]),
        [
            *[shape(value.shape, value.dtype) for value in known],
            shape((share, all_frames, cols), BF16),
            shape((all_frames, all_frames), F32),
        ],
        [*known, *blocks[-2:], edges, edges_other, lhs],
        aliases={0: 0, 1: 1, 2: 2},
    )
    chips = [gram] + [swap(gram, k) for k in range(2, group, 2)]
    grams = chips + [swap(value, 1) for value in chips]
    mix, coef_own, coef_send = call(
        functools.partial(factor_kernel, "tm", count, ranks, pixels),
        [shape((ranks, all_frames), F32), *([shape((TY, frames, ranks), F32)] * 2)],
        [om_all, *grams],
    )
    coef_other = swap(coef_send, group)
    (basis,) = call(basis_kernel, [shape((ranks * share, cols), F32)], [matrix, mix])
    coefficients = jnp.transpose(coef_own + coef_other, (0, 2, 1))[:, None]
    return basis.reshape(ranks, share, cols), coefficients


def solution(mesh):
    in_specs = (P("tm", None, "tile"), P(None, "tile", None, "tm"), P(), P())
    out_specs = (P(None, "tm", "tile"), P(None, "tile", None, "tm"))
    return jax.shard_map(local, mesh=mesh, in_specs=in_specs, out_specs=out_specs, check_vma=False)
```

```python
import functools
import math

import jax
import jax.numpy as jnp
from jax import lax
from jax.experimental import pallas as pl
from jax.experimental.pallas import tpu as pltpu
from jax.sharding import PartitionSpec as P

TY = 2
F32 = jnp.float32
BF16 = jnp.bfloat16


def call(kernel, outs, ins, scratch=(), places=None, grant=40 << 20, aliases=None):
    places = places or [pltpu.VMEM] * len(ins)
    return pl.pallas_call(
        kernel,
        out_shape=outs,
        in_specs=[pl.BlockSpec(memory_space=place) for place in places],
        out_specs=[pl.BlockSpec(memory_space=pltpu.VMEM)] * len(outs),
        scratch_shapes=scratch,
        input_output_aliases=aliases or {},
        compiler_params=pltpu.CompilerParams(vmem_limit_bytes=grant),
        cost_estimate=pl.CostEstimate(flops=0, bytes_accessed=0, transcendentals=0),
    )(*ins)


def toeplitz(tap_row, rows, cols, shift, sign=1):
    offsets = sign * (
        lax.broadcasted_iota(jnp.int32, (rows, cols), 1)
        - lax.broadcasted_iota(jnp.int32, (rows, cols), 0)
    )
    offsets = offsets + shift
    total = jnp.zeros((rows, cols), F32)
    for t in range(tap_row.shape[1]):
        total = jnp.where(offsets == t, tap_row[:, t : t + 1], total)
    return total


def contract(left, right, left_dim, right_dim):
    return lax.dot_general(
        left, right, (((left_dim,), (right_dim,)), ((), ())), preferred_element_type=F32
    )


def split(value):
    high = value.astype(BF16)
    return high, (value - high.astype(F32)).astype(BF16)


def turned(value, shift):
    return pltpu.roll(value, shift % value.shape[1], 1)


def device_at(index, count, shift, flip):
    return (index // 2 + shift) % (count // 2) * 2 + (index % 2 + flip) % 2


def put_rows(out_ref, at, first, size, rows_scr):
    _, frames, cols = out_ref.shape
    start = pl.multiple_of(first * frames, frames)
    block = rows_scr[pl.ds(start, size * frames), :].astype(BF16)
    out_ref[at : at + size] = block.reshape(size, frames, cols)


def put_anchor(out_ref, at, first, size, anchor_scr):
    _, frames, cols = out_ref.shape
    block = anchor_scr[pl.ds(pl.multiple_of(first, size), size), :].astype(BF16)
    out_ref[at : at + size // frames] = block.reshape(size // frames, frames, cols)


def put_omega(out_ref, at, omega):
    frames, cols = out_ref.shape[1], out_ref.shape[2]
    ranks = omega.shape[1]
    out_ref[at, :, 0:ranks] = omega
    out_ref[at, :, ranks:] = jnp.zeros((frames, cols - ranks), BF16)


def put_block(out_ref, at, dest, share, rows_scr, anchor_scr):
    put_rows(out_ref, at, dest * share, share, rows_scr)
    put_anchor(out_ref, at + share, dest * share, share, anchor_scr)


def filter_rows(x_of, halo_of, bx, bh, dy, frames, inner, centre_scr, rows_scr, anchor_scr):
    part, span = dy.shape
    cols = bx.shape[0]

    def mean(value_of):
        total = value_of(0)
        for f in range(1, frames):
            total = total + value_of(f)
        return (total * (1.0 / frames)).astype(BF16)

    def across(block, edge):
        value = contract(block, bx, 1, 0)
        return value if edge is None else value + contract(edge, bh, 0, 0)

    def rows_made(value):
        if part == span:
            return value
        centre_scr[...] = value
        return centre_scr[pl.ds(inner, part), :]

    anchor = mean(x_of)
    edge = None if halo_of is None else mean(halo_of)
    anchor32 = anchor.astype(F32)
    edge32 = None if edge is None else edge.astype(F32)
    high, low = split(across(anchor, edge))
    both = contract(dy, jnp.concatenate([high, low], axis=1), 1, 0)
    anchor_s = rows_made(anchor32) - both[:, :cols] - both[:, cols:]
    anchor_out = anchor_s.astype(BF16).astype(F32)
    anchor_scr[...] = anchor_out
    left_over = anchor_s - anchor_out
    for p in range(frames // 2):
        blocks, smooths = [], []
        for f in (2 * p, 2 * p + 1):
            block = (x_of(f) - anchor32).astype(BF16)
            edge = None if halo_of is None else (halo_of(f) - edge32).astype(BF16)
            smooths.append(across(block, edge).astype(BF16))
            blocks.append(rows_made(block.astype(F32)))
        both = contract(dy, jnp.concatenate(smooths, axis=1), 1, 0)
        for i, f in enumerate((2 * p, 2 * p + 1)):
            value = blocks[i] - both[:, i * cols : (i + 1) * cols] + left_over
            rows_scr[pl.ds(f, part, stride=frames), :] = value


def put_edges(out_ref, index, rows_scr, anchor_scr, share, width, omega):
    _, frames, cols = out_ref.shape
    packed = cols // (2 * width)
    groups = share // packed
    lane = lax.broadcasted_iota(jnp.int32, (frames, cols), 1) // (2 * width)
    start = pl.multiple_of(index * (share * frames), share * frames)
    for group in range(groups):
        tile = jnp.zeros((frames, cols), F32)
        for q in range(packed):
            begin = pl.multiple_of(start + (group * packed + q) * frames, frames)
            value = rows_scr[pl.ds(begin, frames), :]
            tile = jnp.where(lane == q, turned(value, width + 2 * width * q), tile)
        out_ref[group] = tile.astype(BF16)
    first = pl.multiple_of(index * share, share)
    ranks = omega.shape[1]
    tile = jnp.concatenate([omega.astype(F32), jnp.zeros((frames, cols - ranks), F32)], axis=1)
    for q in range(2):
        at = ranks + 2 * width * q
        value = anchor_scr[pl.ds(first + q, share // 2, stride=2), :]
        if share // 2 < frames:
            value = jnp.concatenate([value, jnp.zeros((frames - share // 2, cols), F32)], axis=0)
        tile = jnp.where(lane == at // (2 * width), turned(value, width + at), tile)
    out_ref[groups] = tile.astype(BF16)


def early_kernel(axis, side, count, x_ref, taps_ref, *rest):
    outs, (a_ref, b_ref), scratch = rest[:2], rest[2:4], rest[4:]
    centre_scr, rows_scr, anchor_scr = scratch
    frames, rows, cols = x_ref.shape
    part, span = anchor_scr.shape[0], centre_scr.shape[0]
    share = part // 2
    radius = (taps_ref.shape[1] - 1) // 2
    me = lax.axis_index(axis)
    chip = device_at(me, count, count // 4, 0) // 2
    first = jnp.clip(chip * part - (span - part) // 2, 0, rows - span)
    first = pl.multiple_of(first, 16)
    inner = pl.multiple_of(chip * part - first, 16)
    taps = taps_ref[...].astype(F32)
    bx = toeplitz(taps, cols, cols, radius, -1).astype(BF16)
    dy = toeplitz(taps, part, span, radius - inner).astype(BF16)
    scratch = (centre_scr, rows_scr, anchor_scr)

    def x_of(f):
        return x_ref[f, pl.ds(first, span), :].astype(F32)

    filter_rows(x_of, None, bx, None, dy, frames, inner, *scratch)
    for h, out_ref in enumerate(outs):
        put_block(out_ref, 0, (me + h) % 2, share, rows_scr, anchor_scr)

    row = lax.broadcasted_iota(jnp.int32, (2 * radius, cols), 0)
    col = lax.broadcasted_iota(jnp.int32, (2 * radius, cols), 1)
    right = (row < radius) == (lax.axis_index(side) % 2 == 0)
    wanted = row % radius + jnp.where(right, cols - radius, 0)
    pick = jnp.where(col == wanted, 1.0, 0.0).astype(BF16)
    for f in range(frames):
        both = contract(pick, x_ref[f], 1, 1).astype(BF16)
        a_ref[f] = both[:radius]
        b_ref[f] = both[radius:]


def prepare_kernel(side, x_ref, space_ref, time_ref, om_in, bh_ref, dy_ref, lhs_ref, om_ref, *rest):
    anchor_ref, block_ref, smooth_ref = rest
    om_ref[...] = om_in[...]
    frames, rows, cols = x_ref.shape
    space, time = space_ref[...].astype(F32), time_ref[...].astype(F32)
    radius = (space.shape[1] - 1) // 2
    bx = toeplitz(space, cols, cols, radius, -1).astype(BF16)
    total = jnp.zeros((rows, cols), F32)
    for f in range(frames):
        total = total + x_ref[f].astype(F32)
    anchor = (total * (1.0 / frames)).astype(BF16)
    anchor32 = anchor.astype(F32)
    anchor_ref[...] = anchor32
    smooth_ref[frames] = contract(anchor, bx, 1, 0)
    for f in range(frames):
        block = (x_ref[f].astype(F32) - anchor32).astype(BF16)
        block_ref[f] = block
        smooth_ref[f] = contract(block, bx, 1, 0)
    left = toeplitz(space, radius, cols, 0, -1)
    right = toeplitz(space, radius, cols, radius + cols, -1)
    odd = lax.axis_index(side) % 2 == 1
    bh_ref[0:radius] = jnp.where(odd, left, right).astype(BF16)
    bh_ref[radius:] = jnp.where(odd, right, left).astype(BF16)
    dy_ref[...] = toeplitz(space, rows, rows, radius).astype(BF16)
    all_frames = lhs_ref.shape[0]
    count = (lhs_ref.shape[1] - all_frames) // 2
    frames = all_frames // count
    band = toeplitz(time, all_frames, all_frames, radius)
    ids = lax.broadcasted_iota(jnp.int32, (all_frames, count), 0) // frames
    lane = lax.broadcasted_iota(jnp.int32, (all_frames, count), 1)
    sums = jnp.where(ids == lane, 1.0, 0.0)
    for j in range(count):
        piece = jnp.sum(band[:, j * frames : (j + 1) * frames], axis=1, keepdims=True)
        sums = jnp.where(lane == j, sums - piece, sums)
    high, low = split(sums)
    lhs_ref[:, 0:all_frames] = (-band).astype(BF16)
    lhs_ref[:, all_frames:] = jnp.concatenate([high.astype(F32), low.astype(F32)], 1).astype(BF16)


def spatial_kernel(axis, a_ref, b_ref, bh_ref, dy_ref, om_ref, *rest):
    (anchor_ref, block_ref, smooth_ref), rest = rest[:3], rest[3:]
    outs, edge_refs, (rows_scr, anchor_scr) = rest[:-4], rest[-4:-2], rest[-2:]
    frames, rows, cols = block_ref.shape
    radius = a_ref.shape[1]
    share = (outs[0].shape[0] - 1) * frames // (frames + 1)
    count = rows // share
    me = lax.axis_index(axis)
    bh, dy = bh_ref[...], dy_ref[...]

    def halo(f):
        return jnp.concatenate([a_ref[f].astype(F32), b_ref[f].astype(F32)], axis=0)

    def across(f, edge):
        return smooth_ref[f] + contract(edge, bh, 0, 0)

    total = halo(0)
    for f in range(1, frames):
        total = total + halo(f)
    edge_anchor = (total * (1.0 / frames)).astype(BF16)
    edge32 = edge_anchor.astype(F32)
    high, low = split(across(frames, edge_anchor))
    both = contract(dy, jnp.concatenate([high, low], axis=1), 1, 0)
    anchor_s = anchor_ref[...] - both[:, :cols] - both[:, cols:]
    anchor_out = anchor_s.astype(BF16).astype(F32)
    anchor_scr[...] = anchor_out
    left_over = anchor_s - anchor_out
    for p in range(frames // 2):
        pair = (2 * p, 2 * p + 1)
        smooths = [across(f, (halo(f) - edge32).astype(BF16)).astype(BF16) for f in pair]
        both = contract(dy, jnp.concatenate(smooths, axis=1), 1, 0)
        for i, f in enumerate(pair):
            value = block_ref[f].astype(F32) - both[:, i * cols : (i + 1) * cols] + left_over
            rows_scr[pl.ds(f, rows, stride=frames), :] = value
    early = count // 4
    for (shift, flips), out in zip(message_list(count), outs):
        for i, flip in enumerate(flips):
            dest = device_at(me, count, shift, flip)
            at = i * (share + share // frames + 1)
            put_block(out, at, dest, share, rows_scr, anchor_scr)
            put_omega(out, at + share + share // frames, om_ref[dest // (count // TY)])
    for h, out in enumerate(edge_refs):
        dest = device_at(me, count, early, h)
        omega = om_ref[dest // (count // TY)]
        put_edges(out, dest, rows_scr, anchor_scr, share, radius, omega)


def message_list(count):
    return [(c, (flip,)) for c in range(count // 2) if c != count // 4 for flip in range(2)]


def take_block(data_ref, anchor_ref, ref, at, src):
    share, count, frames, cols = data_ref.shape
    data_ref[:, src] = ref[at : at + share]
    anchor = ref[at + share : at + share + share // frames].reshape(share, cols)
    anchor_ref[pl.ds(src, share, stride=count), :] = anchor.astype(F32)


def take_edges(data_ref, anchor_ref, ref, src, width, ranks):
    share, count, frames, cols = data_ref.shape
    packed = cols // (2 * width)
    groups = share // packed
    lanes = lax.broadcasted_iota(jnp.int32, (frames, cols), 1)
    at_edge = (lanes < width) | (lanes >= cols - width)
    last = ref[groups].astype(F32)
    for q in range(2):
        edge = turned(last, -(width + ranks + 2 * width * q))[: share // 2]
        where = pl.ds(src + q * count, share // 2, stride=2 * count)
        old = anchor_ref[where, :]
        anchor_ref[where, :] = jnp.where(at_edge[: share // 2], edge, old)
    for group in range(groups):
        tile = ref[group].astype(F32)
        for q in range(packed):
            r = group * packed + q
            edge = turned(tile, -(width + 2 * width * q))
            value = jnp.where(at_edge, edge, data_ref[r, src].astype(F32))
            data_ref[r, src] = value.astype(BF16)


def gather_kernel(axis, places, *refs):
    blocks, mains, (data_ref, anchor_ref, om_ref) = refs[:-5], refs[-5:-3], refs[-3:]
    share, count, frames, _ = data_ref.shape
    slots = share + share // frames
    me = lax.axis_index(axis)
    for (shift, flip), ref in zip(places, blocks):
        src = device_at(me, count, -shift, flip)
        take_block(data_ref, anchor_ref, ref, 0, src)
        om_ref[src] = ref[slots]
    for h, ref in enumerate(mains):
        take_block(data_ref, anchor_ref, ref, 0, device_at(me, count, -(count // 4), h))


def temporal_kernel(axis, width, ranks, places, *refs):
    blocks, edge_refs, lhs_ref = refs[3:-8], refs[-8:-6], refs[-6]
    data_ref, anchor_ref, om_ref, m_ref, gram_ref = refs[-5:]
    share, count, frames, cols = data_ref.shape
    all_frames = count * frames
    slots = share + share // frames
    me = lax.axis_index(axis)
    for (shift, flip), ref in zip(places, blocks):
        src = device_at(me, count, -shift, flip)
        take_block(data_ref, anchor_ref, ref, 0, src)
        om_ref[src] = ref[slots]
    for h, ref in enumerate(edge_refs):
        src = device_at(me, count, -(count // 4), h)
        take_edges(data_ref, anchor_ref, ref, src, width, ranks)
        om_ref[src] = ref[ref.shape[0] - 1]
    lhs = lhs_ref[...]
    gram = jnp.zeros((all_frames, all_frames), F32)
    for p in range(share // 2):
        blocks, feeds = [], []
        for r in (2 * p, 2 * p + 1):
            block = data_ref[r].reshape(all_frames, cols)
            anchor = anchor_ref[r * count : (r + 1) * count, :]
            blocks.append(block)
            feeds.append(
                jnp.concatenate([block, jnp.concatenate([anchor, anchor], 0).astype(BF16)], axis=0)
            )
        low = contract(lhs, jnp.concatenate(feeds, axis=1), 1, 0)
        value = (jnp.concatenate(blocks, axis=1).astype(F32) + low).astype(BF16)
        m_ref[2 * p] = value[:, :cols]
        m_ref[2 * p + 1] = value[:, cols:]
        gram = gram + contract(value, value, 1, 1)
    gram_ref[...] = gram


def exact(left, right, left_dim, right_dim):
    return lax.dot_general(
        left,
        right,
        (((left_dim,), (right_dim,)), ((), ())),
        precision=lax.Precision.HIGHEST,
        preferred_element_type=F32,
    )


def whiten(gram, *others):
    size = gram.shape[0]
    ids = lax.broadcasted_iota(jnp.int32, (size, 128), 0)
    work = [jnp.concatenate([gram, jnp.zeros((size, 128 - size), F32)], axis=1), *others]
    scale = jnp.zeros((size, 128), F32)
    panel = 16
    for start in range(0, size, panel):
        cols = [
            jnp.broadcast_to(work[0][:, j : j + 1], (size, 128)) for j in range(start, start + panel)
        ]
        for j in range(start, start + panel):
            inverse = 1.0 / cols[j - start][j : j + 1]
            factor = jnp.where(ids > j, cols[j - start] * inverse, 0.0)
            scale = jnp.where(ids == j, inverse, scale)
            for m in range(j - start + 1, panel):
                cols[m] = cols[m] - factor * cols[m][j : j + 1]
            for i in range(len(work)):
                value = work[i]
                width = value.shape[1]
                parts = [
                    value[:, c : c + 128] - factor * value[j : j + 1, c : c + 128]
                    for c in range(0, width, 128)
                ]
                work[i] = parts[0] if len(parts) == 1 else jnp.concatenate(parts, axis=1)
    scale = jnp.sqrt(scale)
    results = []
    for value in work[1:]:
        parts = [value[:, c : c + 128] * scale for c in range(0, value.shape[1], 128)]
        results.append(parts[0] if len(parts) == 1 else jnp.concatenate(parts, axis=1))
    return results


def factor_kernel(axis, count, ranks, pixels, om_ref, *refs):
    grams, (mix_ref, own_ref, send_ref, coef_scr) = refs[:-4], refs[-4:]
    frames = own_ref.shape[1]
    all_frames = grams[0].shape[0]
    me = lax.axis_index(axis)
    gram = grams[0][...]
    for other in grams[1:]:
        gram = gram + other[...]
    omega = om_ref[...].reshape(all_frames, om_ref.shape[2]).astype(F32).T[:ranks]
    sketch = exact(omega, gram, 1, 0)
    (load,) = whiten(exact(sketch, omega, 1, 1), sketch)
    back = exact(load, gram, 1, 0)
    mix, coef = whiten(exact(back, load, 1, 1), load, back)
    mix_ref[...] = mix * math.sqrt(pixels)
    coef_scr[...] = coef.T
    for ref, who in ((own_ref, me), (send_ref, me ^ (count // TY))):
        ref[...] = jnp.zeros_like(ref)
        start = pl.multiple_of(who * frames, frames)
        ref[me // (count // TY)] = coef_scr[pl.ds(start, frames), :]


def basis_kernel(m_ref, mix_ref, out_ref):
    share, _, cols = m_ref.shape
    ranks = mix_ref.shape[0]
    high, low = split(mix_ref[...])
    lhs = jnp.concatenate([high, low], axis=0)
    for p in range(share // 2):
        data = jnp.concatenate([m_ref[2 * p], m_ref[2 * p + 1]], axis=1)
        both = contract(lhs, data, 1, 0)
        value = both[:ranks] + both[ranks:]
        for i in range(2):
            out_ref[pl.ds(2 * p + i, ranks, stride=share), :] = value[:, i * cols : (i + 1) * cols]


def local(movie, omega, time_taps, space_taps):
    frames, rows, cols = movie.shape
    radius = (space_taps.shape[0] - 1) // 2
    count = lax.axis_size("tm")
    tiles = lax.axis_size("tile")
    ranks = omega.shape[2]
    share = rows // count
    all_frames = frames * count
    group = count // TY
    pixels = (rows // TY) * cols
    early = count // 4
    packed = cols // (2 * radius)
    slots = share + share // frames

    def shape(dims, dtype):
        return jax.ShapeDtypeStruct(dims, dtype)

    def swap(value, k):
        return lax.ppermute(value, "tm", [(i, i ^ k) for i in range(count)])

    def send(value, shift, flip):
        return lax.ppermute(value, "tm", [(i, device_at(i, count, shift, flip)) for i in range(count)])

    space_row, time_row = space_taps[None], time_taps[None]
    part = 2 * share
    span = part + 32
    *mains, side_a, side_b = call(
        functools.partial(early_kernel, "tm", "tile", count),
        [
            *([shape((slots, frames, cols), BF16)] * 2),
            *([shape((frames, radius, rows), BF16)] * 2),
        ],
        [movie, space_row],
        [
            pltpu.VMEM((span, cols), F32),
            pltpu.VMEM((part * frames, cols), F32),
            pltpu.VMEM((part, cols), F32),
        ],
    )
    mains = [send(value, early, h) for h, value in enumerate(mains)]
    pairs = [(i, i ^ 1) for i in range(tiles)]
    side_a = lax.ppermute(side_a, "tile", pairs)
    pairs = [(i, i + 1) for i in range(1, tiles - 1, 2)]
    side_b = lax.ppermute(side_b, "tile", pairs + [(j, i) for i, j in pairs])
    om = jnp.transpose(omega[:, 0], (0, 2, 1))
    bh, dy, lhs, om, *prepared = call(
        functools.partial(prepare_kernel, "tile"),
        [
            shape((2 * radius, cols), BF16),
            shape((rows, rows), BF16),
            shape((all_frames, all_frames + 2 * count), BF16),
            shape(om.shape, om.dtype),
            shape((rows, cols), F32),
            shape(movie.shape, BF16),
            shape((frames + 1, rows, cols), F32),
        ],
        [movie, space_row, time_row, om],
    )
    listed = message_list(count)
    *parts, edges, edges_other = call(
        functools.partial(spatial_kernel, "tm"),
        [
            *[shape((len(flips) * (slots + 1), frames, cols), BF16) for _, flips in listed],
            *([shape((share // packed + 1, frames, cols), BF16)] * 2),
        ],
        [side_a, side_b, bh, dy, om, *prepared],
        [pltpu.VMEM((rows * frames, cols), F32), pltpu.VMEM((rows, cols), F32)],
    )
    def after(value, *others):
        return lax.optimization_barrier((value, *others))[0]

    parts[-1] = after(parts[-1], *mains)
    blocks = [parts[0]] + [
        send(value, shift, flip) for (shift, (flip,)), value in zip(listed[1:], parts[1:])
    ]
    edges = send(after(edges, blocks[1]), early, 0)
    edges_other = send(after(edges_other, blocks[1]), early, 1)
    places = [(shift, flip) for shift, flips in listed for flip in flips]
    known = call(
        functools.partial(gather_kernel, "tm", places[:-2]),
        [
            shape((share, count, frames, cols), BF16),
            shape((share * count, cols), F32),
            shape((count, frames, cols), BF16),
        ],
        [*blocks[:-2], *mains],
    )
    _, _, om_all, matrix, gram = call(
        functools.partial(temporal_kernel, "tm", radius, ranks, places[-2:]),
        [
            *[shape(value.shape, value.dtype) for value in known],
            shape((share, all_frames, cols), BF16),
            shape((all_frames, all_frames), F32),
        ],
        [*known, *blocks[-2:], edges, edges_other, lhs],
        aliases={0: 0, 1: 1, 2: 2},
    )
    chips = [gram] + [swap(gram, k) for k in range(2, group, 2)]
    grams = chips + [swap(value, 1) for value in chips]
    mix, coef_own, coef_send = call(
        functools.partial(factor_kernel, "tm", count, ranks, pixels),
        [shape((ranks, all_frames), F32), *([shape((TY, frames, ranks), F32)] * 2)],
        [om_all, *grams],
        [pltpu.VMEM((all_frames, ranks), F32)],
    )
    coef_other = swap(coef_send, group)
    (basis,) = call(basis_kernel, [shape((ranks * share, cols), F32)], [matrix, mix])
    coefficients = jnp.transpose(coef_own + coef_other, (0, 2, 1))[:, None]
    return basis.reshape(ranks, share, cols), coefficients


def solution(mesh):
    in_specs = (P("tm", None, "tile"), P(None, "tile", None, "tm"), P(), P())
    out_specs = (P(None, "tm", "tile"), P(None, "tile", None, "tm"))
    return jax.shard_map(local, mesh=mesh, in_specs=in_specs, out_specs=out_specs, check_vma=False)
```

```python
import functools
import math

import jax
import jax.numpy as jnp
from jax import lax
from jax.experimental import pallas as pl
from jax.experimental.pallas import tpu as pltpu
from jax.sharding import PartitionSpec as P

TY = 2
F32 = jnp.float32
BF16 = jnp.bfloat16


def call(kernel, outs, ins, scratch=(), places=None, grant=40 << 20, aliases=None):
    places = places or [pltpu.VMEM] * len(ins)
    return pl.pallas_call(
        kernel,
        out_shape=outs,
        in_specs=[pl.BlockSpec(memory_space=place) for place in places],
        out_specs=[pl.BlockSpec(memory_space=pltpu.VMEM)] * len(outs),
        scratch_shapes=scratch,
        input_output_aliases=aliases or {},
        compiler_params=pltpu.CompilerParams(vmem_limit_bytes=grant),
        cost_estimate=pl.CostEstimate(flops=0, bytes_accessed=0, transcendentals=0),
    )(*ins)


def toeplitz(tap_row, rows, cols, shift, sign=1):
    offsets = sign * (
        lax.broadcasted_iota(jnp.int32, (rows, cols), 1)
        - lax.broadcasted_iota(jnp.int32, (rows, cols), 0)
    )
    offsets = offsets + shift
    total = jnp.zeros((rows, cols), F32)
    for t in range(tap_row.shape[1]):
        total = jnp.where(offsets == t, tap_row[:, t : t + 1], total)
    return total


def contract(left, right, left_dim, right_dim):
    return lax.dot_general(
        left, right, (((left_dim,), (right_dim,)), ((), ())), preferred_element_type=F32
    )


def split(value):
    high = value.astype(BF16)
    return high, (value - high.astype(F32)).astype(BF16)


def turned(value, shift):
    return pltpu.roll(value, shift % value.shape[1], 1)


def device_at(index, count, shift, flip):
    return (index // 2 + shift) % (count // 2) * 2 + (index % 2 + flip) % 2


def put_rows(out_ref, at, first, size, rows_scr):
    _, frames, cols = out_ref.shape
    start = pl.multiple_of(first * frames, frames)
    block = rows_scr[pl.ds(start, size * frames), :].astype(BF16)
    out_ref[at : at + size] = block.reshape(size, frames, cols)


def put_anchor(out_ref, at, first, size, anchor_scr):
    _, frames, cols = out_ref.shape
    block = anchor_scr[pl.ds(pl.multiple_of(first, size), size), :].astype(BF16)
    out_ref[at : at + size // frames] = block.reshape(size // frames, frames, cols)


def put_omega(out_ref, at, omega):
    frames, cols = out_ref.shape[1], out_ref.shape[2]
    ranks = omega.shape[1]
    out_ref[at, :, 0:ranks] = omega
    out_ref[at, :, ranks:] = jnp.zeros((frames, cols - ranks), BF16)


def put_block(out_ref, at, dest, share, rows_scr, anchor_scr):
    put_rows(out_ref, at, dest * share, share, rows_scr)
    put_anchor(out_ref, at + share, dest * share, share, anchor_scr)


def put_edges(out_ref, index, rows_scr, anchor_scr, share, width, omega):
    _, frames, cols = out_ref.shape
    packed = cols // (2 * width)
    groups = share // packed
    lane = lax.broadcasted_iota(jnp.int32, (frames, cols), 1) // (2 * width)
    start = pl.multiple_of(index * (share * frames), share * frames)
    for group in range(groups):
        tile = jnp.zeros((frames, cols), F32)
        for q in range(packed):
            begin = pl.multiple_of(start + (group * packed + q) * frames, frames)
            value = rows_scr[pl.ds(begin, frames), :]
            tile = jnp.where(lane == q, turned(value, width + 2 * width * q), tile)
        out_ref[group] = tile.astype(BF16)
    first = pl.multiple_of(index * share, share)
    ranks = omega.shape[1]
    tile = jnp.concatenate([omega.astype(F32), jnp.zeros((frames, cols - ranks), F32)], axis=1)
    for q in range(2):
        at = ranks + 2 * width * q
        value = anchor_scr[pl.ds(first + q, share // 2, stride=2), :]
        if share // 2 < frames:
            value = jnp.concatenate([value, jnp.zeros((frames - share // 2, cols), F32)], axis=0)
        tile = jnp.where(lane == at // (2 * width), turned(value, width + at), tile)
    out_ref[groups] = tile.astype(BF16)


def early_kernel(axis, side, count, x_ref, taps_ref, *rest):
    outs, (a_ref, b_ref), scratch = rest[:2], rest[2:4], rest[4:]
    centre_scr, rows_scr, anchor_scr = scratch
    frames, rows, cols = x_ref.shape
    part, span = anchor_scr.shape[0], centre_scr.shape[0]
    share = part // 2
    radius = (taps_ref.shape[1] - 1) // 2
    me = lax.axis_index(axis)
    chip = device_at(me, count, count // 4, 0) // 2
    first = jnp.clip(chip * part - (span - part) // 2, 0, rows - span)
    first = pl.multiple_of(first, 16)
    inner = pl.multiple_of(chip * part - first, 16)
    taps = taps_ref[...].astype(F32)
    bx = toeplitz(taps, cols, cols, radius, -1).astype(BF16)
    dy = toeplitz(taps, part, span, radius - inner).astype(BF16)
    middle = pl.multiple_of(chip * part, part)
    total = jnp.zeros((span, cols), F32)
    for f in range(frames):
        total = total + x_ref[f, pl.ds(first, span), :].astype(F32)
    anchor = (total * (1.0 / frames)).astype(BF16)
    anchor32 = anchor.astype(F32)
    centre_scr[...] = anchor32
    centre = centre_scr[pl.ds(inner, part), :]
    blocks = [anchor]
    for f in range(frames):
        blocks.append((x_ref[f, pl.ds(first, span), :].astype(F32) - anchor32).astype(BF16))
    smooth = contract(jnp.concatenate(blocks, axis=0), bx, 1, 0)
    high, low = split(smooth[:span])
    both = contract(dy, jnp.concatenate([high, low], axis=1), 1, 0)
    anchor_s = centre - both[:, :cols] - both[:, cols:]
    anchor_out = anchor_s.astype(BF16).astype(F32)
    anchor_scr[...] = anchor_out
    left_over = anchor_s - anchor_out
    for p in range(frames // 2):
        pair = (2 * p, 2 * p + 1)
        smooths = [smooth[(f + 1) * span : (f + 2) * span].astype(BF16) for f in pair]
        both = contract(dy, jnp.concatenate(smooths, axis=1), 1, 0)
        for i, f in enumerate(pair):
            block = x_ref[f, pl.ds(middle, part), :].astype(F32) - centre
            block = block.astype(BF16).astype(F32)
            value = block - both[:, i * cols : (i + 1) * cols] + left_over
            rows_scr[pl.ds(f, part, stride=frames), :] = value
    for h, out_ref in enumerate(outs):
        put_block(out_ref, 0, (me + h) % 2, share, rows_scr, anchor_scr)

    row = lax.broadcasted_iota(jnp.int32, (2 * radius, cols), 0)
    col = lax.broadcasted_iota(jnp.int32, (2 * radius, cols), 1)
    right = (row < radius) == (lax.axis_index(side) % 2 == 0)
    wanted = row % radius + jnp.where(right, cols - radius, 0)
    pick = jnp.where(col == wanted, 1.0, 0.0).astype(BF16)
    for f in range(frames):
        both = contract(pick, x_ref[f], 1, 1).astype(BF16)
        a_ref[f] = both[:radius]
        b_ref[f] = both[radius:]


def prepare_kernel(side, x_ref, space_ref, time_ref, om_in, bh_ref, dy_ref, lhs_ref, om_ref, *rest):
    anchor_ref, block_ref, smooth_ref = rest
    om_ref[...] = om_in[...]
    frames, rows, cols = x_ref.shape
    space, time = space_ref[...].astype(F32), time_ref[...].astype(F32)
    radius = (space.shape[1] - 1) // 2
    bx = toeplitz(space, cols, cols, radius, -1).astype(BF16)
    total = jnp.zeros((rows, cols), F32)
    for f in range(frames):
        total = total + x_ref[f].astype(F32)
    anchor = (total * (1.0 / frames)).astype(BF16)
    anchor32 = anchor.astype(F32)
    anchor_ref[...] = anchor32
    smooth_ref[frames] = contract(anchor, bx, 1, 0)
    for f in range(frames):
        block = (x_ref[f].astype(F32) - anchor32).astype(BF16)
        block_ref[f] = block
        smooth_ref[f] = contract(block, bx, 1, 0)
    left = toeplitz(space, radius, cols, 0, -1)
    right = toeplitz(space, radius, cols, radius + cols, -1)
    odd = lax.axis_index(side) % 2 == 1
    bh_ref[0:radius] = jnp.where(odd, left, right).astype(BF16)
    bh_ref[radius:] = jnp.where(odd, right, left).astype(BF16)
    dy_ref[...] = toeplitz(space, rows, rows, radius).astype(BF16)
    all_frames = lhs_ref.shape[0]
    count = (lhs_ref.shape[1] - all_frames) // 2
    frames = all_frames // count
    band = toeplitz(time, all_frames, all_frames, radius)
    ids = lax.broadcasted_iota(jnp.int32, (all_frames, count), 0) // frames
    lane = lax.broadcasted_iota(jnp.int32, (all_frames, count), 1)
    sums = jnp.where(ids == lane, 1.0, 0.0)
    for j in range(count):
        piece = jnp.sum(band[:, j * frames : (j + 1) * frames], axis=1, keepdims=True)
        sums = jnp.where(lane == j, sums - piece, sums)
    high, low = split(sums)
    lhs_ref[:, 0:all_frames] = (-band).astype(BF16)
    lhs_ref[:, all_frames:] = jnp.concatenate([high.astype(F32), low.astype(F32)], 1).astype(BF16)


def spatial_kernel(axis, a_ref, b_ref, bh_ref, dy_ref, om_ref, *rest):
    (anchor_ref, block_ref, smooth_ref), rest = rest[:3], rest[3:]
    outs, edge_refs, (rows_scr, anchor_scr) = rest[:-4], rest[-4:-2], rest[-2:]
    frames, rows, cols = block_ref.shape
    radius = a_ref.shape[1]
    share = (outs[0].shape[0] - 1) * frames // (frames + 1)
    count = rows // share
    me = lax.axis_index(axis)
    bh, dy = bh_ref[...], dy_ref[...]

    def halo(f):
        return jnp.concatenate([a_ref[f].astype(F32), b_ref[f].astype(F32)], axis=0)

    def across(f, edge):
        return smooth_ref[f] + contract(edge, bh, 0, 0)

    total = halo(0)
    for f in range(1, frames):
        total = total + halo(f)
    edge_anchor = (total * (1.0 / frames)).astype(BF16)
    edge32 = edge_anchor.astype(F32)
    high, low = split(across(frames, edge_anchor))
    both = contract(dy, jnp.concatenate([high, low], axis=1), 1, 0)
    anchor_s = anchor_ref[...] - both[:, :cols] - both[:, cols:]
    anchor_out = anchor_s.astype(BF16).astype(F32)
    anchor_scr[...] = anchor_out
    left_over = anchor_s - anchor_out
    for p in range(frames // 2):
        pair = (2 * p, 2 * p + 1)
        smooths = [across(f, (halo(f) - edge32).astype(BF16)).astype(BF16) for f in pair]
        both = contract(dy, jnp.concatenate(smooths, axis=1), 1, 0)
        for i, f in enumerate(pair):
            value = block_ref[f].astype(F32) - both[:, i * cols : (i + 1) * cols] + left_over
            rows_scr[pl.ds(f, rows, stride=frames), :] = value
    early = count // 4
    for (shift, flips), out in zip(message_list(count), outs):
        for i, flip in enumerate(flips):
            dest = device_at(me, count, shift, flip)
            at = i * (share + share // frames + 1)
            put_block(out, at, dest, share, rows_scr, anchor_scr)
            put_omega(out, at + share + share // frames, om_ref[dest // (count // TY)])
    for h, out in enumerate(edge_refs):
        dest = device_at(me, count, early, h)
        omega = om_ref[dest // (count // TY)]
        put_edges(out, dest, rows_scr, anchor_scr, share, radius, omega)


def message_list(count):
    return [(c, (flip,)) for c in range(count // 2) if c != count // 4 for flip in range(2)]


def take_block(data_ref, anchor_ref, ref, at, src):
    share, count, frames, cols = data_ref.shape
    data_ref[:, src] = ref[at : at + share]
    anchor = ref[at + share : at + share + share // frames].reshape(share, cols)
    anchor_ref[pl.ds(src, share, stride=count), :] = anchor.astype(F32)


def take_edges(data_ref, anchor_ref, ref, src, width, ranks):
    share, count, frames, cols = data_ref.shape
    packed = cols // (2 * width)
    groups = share // packed
    lanes = lax.broadcasted_iota(jnp.int32, (frames, cols), 1)
    at_edge = (lanes < width) | (lanes >= cols - width)
    last = ref[groups].astype(F32)
    for q in range(2):
        edge = turned(last, -(width + ranks + 2 * width * q))[: share // 2]
        where = pl.ds(src + q * count, share // 2, stride=2 * count)
        old = anchor_ref[where, :]
        anchor_ref[where, :] = jnp.where(at_edge[: share // 2], edge, old)
    for group in range(groups):
        tile = ref[group].astype(F32)
        for q in range(packed):
            r = group * packed + q
            edge = turned(tile, -(width + 2 * width * q))
            value = jnp.where(at_edge, edge, data_ref[r, src].astype(F32))
            data_ref[r, src] = value.astype(BF16)


def gather_kernel(axis, places, *refs):
    blocks, mains, (data_ref, anchor_ref, om_ref) = refs[:-5], refs[-5:-3], refs[-3:]
    share, count, frames, _ = data_ref.shape
    slots = share + share // frames
    me = lax.axis_index(axis)
    for (shift, flip), ref in zip(places, blocks):
        src = device_at(me, count, -shift, flip)
        take_block(data_ref, anchor_ref, ref, 0, src)
        om_ref[src] = ref[slots]
    for h, ref in enumerate(mains):
        take_block(data_ref, anchor_ref, ref, 0, device_at(me, count, -(count // 4), h))


def temporal_kernel(axis, width, ranks, places, *refs):
    blocks, edge_refs, lhs_ref = refs[3:-9], refs[-9:-7], refs[-7]
    data_ref, anchor_ref, om_ref, m_ref, gram_ref, turned_ref = refs[-6:]
    share, count, frames, cols = data_ref.shape
    all_frames = count * frames
    slots = share + share // frames
    me = lax.axis_index(axis)
    for (shift, flip), ref in zip(places, blocks):
        src = device_at(me, count, -shift, flip)
        take_block(data_ref, anchor_ref, ref, 0, src)
        om_ref[src] = ref[slots]
    for h, ref in enumerate(edge_refs):
        src = device_at(me, count, -(count // 4), h)
        take_edges(data_ref, anchor_ref, ref, src, width, ranks)
        om_ref[src] = ref[ref.shape[0] - 1]
    lhs = lhs_ref[...]
    gram = jnp.zeros((all_frames, all_frames), F32)
    for p in range(share // 2):
        blocks, feeds = [], []
        for r in (2 * p, 2 * p + 1):
            block = data_ref[r].reshape(all_frames, cols)
            anchor = anchor_ref[r * count : (r + 1) * count, :]
            blocks.append(block)
            feeds.append(
                jnp.concatenate([block, jnp.concatenate([anchor, anchor], 0).astype(BF16)], axis=0)
            )
        low = contract(lhs, jnp.concatenate(feeds, axis=1), 1, 0)
        value = (jnp.concatenate(blocks, axis=1).astype(F32) + low).astype(BF16)
        m_ref[2 * p] = value[:, :cols]
        m_ref[2 * p + 1] = value[:, cols:]
        gram = gram + contract(value, value, 1, 1)
    gram_ref[...] = gram
    omega = om_ref[...].reshape(all_frames, cols).astype(F32)
    turned_ref[...] = omega.T[:ranks]


def exact(left, right, left_dim, right_dim):
    return lax.dot_general(
        left,
        right,
        (((left_dim,), (right_dim,)), ((), ())),
        precision=lax.Precision.HIGHEST,
        preferred_element_type=F32,
    )


def whiten(gram, *others):
    size = gram.shape[0]
    ids = lax.broadcasted_iota(jnp.int32, (size, 128), 0)
    work = [jnp.concatenate([gram, jnp.zeros((size, 128 - size), F32)], axis=1), *others]
    scale = jnp.zeros((size, 128), F32)
    panel = 16
    for start in range(0, size, panel):
        cols = [
            jnp.broadcast_to(work[0][:, j : j + 1], (size, 128)) for j in range(start, start + panel)
        ]
        for j in range(start, start + panel):
            inverse = 1.0 / cols[j - start][j : j + 1]
            factor = jnp.where(ids > j, cols[j - start] * inverse, 0.0)
            scale = jnp.where(ids == j, inverse, scale)
            for m in range(j - start + 1, panel):
                cols[m] = cols[m] - factor * cols[m][j : j + 1]
            for i in range(len(work)):
                value = work[i]
                width = value.shape[1]
                parts = [
                    value[:, c : c + 128] - factor * value[j : j + 1, c : c + 128]
                    for c in range(0, width, 128)
                ]
                work[i] = parts[0] if len(parts) == 1 else jnp.concatenate(parts, axis=1)
    scale = jnp.sqrt(scale)
    results = []
    for value in work[1:]:
        parts = [value[:, c : c + 128] * scale for c in range(0, value.shape[1], 128)]
        results.append(parts[0] if len(parts) == 1 else jnp.concatenate(parts, axis=1))
    return results


def factor_kernel(axis, count, ranks, pixels, om_ref, *refs):
    grams, (mix_ref, own_ref, send_ref, coef_scr) = refs[:-4], refs[-4:]
    frames = own_ref.shape[1]
    all_frames = grams[0].shape[0]
    me = lax.axis_index(axis)
    gram = grams[0][...]
    for other in grams[1:]:
        gram = gram + other[...]
    omega = om_ref[...]
    sketch = exact(omega, gram, 1, 0)
    (load,) = whiten(exact(sketch, omega, 1, 1), sketch)
    back = exact(load, gram, 1, 0)
    mix, coef = whiten(exact(back, load, 1, 1), load, back)
    mix_ref[...] = mix * math.sqrt(pixels)
    coef_scr[...] = coef.T
    for ref, who in ((own_ref, me), (send_ref, me ^ (count // TY))):
        ref[...] = jnp.zeros_like(ref)
        start = pl.multiple_of(who * frames, frames)
        ref[me // (count // TY)] = coef_scr[pl.ds(start, frames), :]


def basis_kernel(m_ref, mix_ref, out_ref):
    share, _, cols = m_ref.shape
    ranks = mix_ref.shape[0]
    high, low = split(mix_ref[...])
    lhs = jnp.concatenate([high, low], axis=0)
    for p in range(share // 2):
        data = jnp.concatenate([m_ref[2 * p], m_ref[2 * p + 1]], axis=1)
        both = contract(lhs, data, 1, 0)
        value = both[:ranks] + both[ranks:]
        for i in range(2):
            out_ref[pl.ds(2 * p + i, ranks, stride=share), :] = value[:, i * cols : (i + 1) * cols]


def local(movie, omega, time_taps, space_taps):
    frames, rows, cols = movie.shape
    radius = (space_taps.shape[0] - 1) // 2
    count = lax.axis_size("tm")
    tiles = lax.axis_size("tile")
    ranks = omega.shape[2]
    share = rows // count
    all_frames = frames * count
    group = count // TY
    pixels = (rows // TY) * cols
    early = count // 4
    packed = cols // (2 * radius)
    slots = share + share // frames

    def shape(dims, dtype):
        return jax.ShapeDtypeStruct(dims, dtype)

    def swap(value, k):
        return lax.ppermute(value, "tm", [(i, i ^ k) for i in range(count)])

    def send(value, shift, flip):
        return lax.ppermute(value, "tm", [(i, device_at(i, count, shift, flip)) for i in range(count)])

    space_row, time_row = space_taps[None], time_taps[None]
    part = 2 * share
    span = part + 32
    *mains, side_a, side_b = call(
        functools.partial(early_kernel, "tm", "tile", count),
        [
            *([shape((slots, frames, cols), BF16)] * 2),
            *([shape((frames, radius, rows), BF16)] * 2),
        ],
        [movie, space_row],
        [
            pltpu.VMEM((span, cols), F32),
            pltpu.VMEM((part * frames, cols), F32),
            pltpu.VMEM((part, cols), F32),
        ],
    )
    mains = [send(value, early, h) for h, value in enumerate(mains)]
    pairs = [(i, i ^ 1) for i in range(tiles)]
    side_a = lax.ppermute(side_a, "tile", pairs)
    pairs = [(i, i + 1) for i in range(1, tiles - 1, 2)]
    side_b = lax.ppermute(side_b, "tile", pairs + [(j, i) for i, j in pairs])
    om = jnp.transpose(omega[:, 0], (0, 2, 1))
    bh, dy, lhs, om, *prepared = call(
        functools.partial(prepare_kernel, "tile"),
        [
            shape((2 * radius, cols), BF16),
            shape((rows, rows), BF16),
            shape((all_frames, all_frames + 2 * count), BF16),
            shape(om.shape, om.dtype),
            shape((rows, cols), F32),
            shape(movie.shape, BF16),
            shape((frames + 1, rows, cols), F32),
        ],
        [movie, space_row, time_row, om],
    )
    listed = message_list(count)
    *parts, edges, edges_other = call(
        functools.partial(spatial_kernel, "tm"),
        [
            *[shape((len(flips) * (slots + 1), frames, cols), BF16) for _, flips in listed],
            *([shape((share // packed + 1, frames, cols), BF16)] * 2),
        ],
        [side_a, side_b, bh, dy, om, *prepared],
        [pltpu.VMEM((rows * frames, cols), F32), pltpu.VMEM((rows, cols), F32)],
    )
    def after(value, *others):
        return lax.optimization_barrier((value, *others))[0]

    parts[-1] = after(parts[-1], *mains)
    blocks = [parts[0]] + [
        send(value, shift, flip) for (shift, (flip,)), value in zip(listed[1:], parts[1:])
    ]
    edges = send(after(edges, blocks[1]), early, 0)
    edges_other = send(after(edges_other, blocks[1]), early, 1)
    places = [(shift, flip) for shift, flips in listed for flip in flips]
    known = call(
        functools.partial(gather_kernel, "tm", places[:-2]),
        [
            shape((share, count, frames, cols), BF16),
            shape((share * count, cols), F32),
            shape((count, frames, cols), BF16),
        ],
        [*blocks[:-2], *mains],
    )
    *_, matrix, gram, om_all = call(
        functools.partial(temporal_kernel, "tm", radius, ranks, places[-2:]),
        [
            *[shape(value.shape, value.dtype) for value in known],
            shape((share, all_frames, cols), BF16),
            shape((all_frames, all_frames), F32),
            shape((ranks, all_frames), F32),
        ],
        [*known, *blocks[-2:], edges, edges_other, lhs],
        aliases={0: 0, 1: 1, 2: 2},
    )
    chips = [gram] + [swap(gram, k) for k in range(2, group, 2)]
    grams = chips + [swap(value, 1) for value in chips]
    mix, coef_own, coef_send = call(
        functools.partial(factor_kernel, "tm", count, ranks, pixels),
        [shape((ranks, all_frames), F32), *([shape((TY, frames, ranks), F32)] * 2)],
        [om_all, *grams],
        [pltpu.VMEM((all_frames, ranks), F32)],
    )
    coef_other = swap(coef_send, group)
    (basis,) = call(basis_kernel, [shape((ranks * share, cols), F32)], [matrix, mix])
    coefficients = jnp.transpose(coef_own + coef_other, (0, 2, 1))[:, None]
    return basis.reshape(ranks, share, cols), coefficients


def solution(mesh):
    in_specs = (P("tm", None, "tile"), P(None, "tile", None, "tm"), P(), P())
    out_specs = (P(None, "tm", "tile"), P(None, "tile", None, "tm"))
    return jax.shard_map(local, mesh=mesh, in_specs=in_specs, out_specs=out_specs, check_vma=False)
```

```python
import functools
import math

import jax
import jax.numpy as jnp
from jax import lax
from jax.experimental import pallas as pl
from jax.experimental.pallas import tpu as pltpu
from jax.sharding import PartitionSpec as P

TY = 2
F32 = jnp.float32
BF16 = jnp.bfloat16


def call(kernel, outs, ins, scratch=(), places=None, grant=40 << 20, aliases=None):
    places = places or [pltpu.VMEM] * len(ins)
    return pl.pallas_call(
        kernel,
        out_shape=outs,
        in_specs=[pl.BlockSpec(memory_space=place) for place in places],
        out_specs=[pl.BlockSpec(memory_space=pltpu.VMEM)] * len(outs),
        scratch_shapes=scratch,
        input_output_aliases=aliases or {},
        compiler_params=pltpu.CompilerParams(vmem_limit_bytes=grant),
        cost_estimate=pl.CostEstimate(flops=0, bytes_accessed=0, transcendentals=0),
    )(*ins)


def toeplitz(tap_row, rows, cols, shift, sign=1):
    offsets = sign * (
        lax.broadcasted_iota(jnp.int32, (rows, cols), 1)
        - lax.broadcasted_iota(jnp.int32, (rows, cols), 0)
    )
    offsets = offsets + shift
    total = jnp.zeros((rows, cols), F32)
    for t in range(tap_row.shape[1]):
        total = jnp.where(offsets == t, tap_row[:, t : t + 1], total)
    return total


def contract(left, right, left_dim, right_dim):
    return lax.dot_general(
        left, right, (((left_dim,), (right_dim,)), ((), ())), preferred_element_type=F32
    )


def split(value):
    high = value.astype(BF16)
    return high, (value - high.astype(F32)).astype(BF16)


def turned(value, shift):
    return pltpu.roll(value, shift % value.shape[1], 1)


def device_at(index, count, shift, flip):
    return (index // 2 + shift) % (count // 2) * 2 + (index % 2 + flip) % 2


def put_rows(out_ref, at, first, size, rows_scr):
    _, frames, cols = out_ref.shape
    start = pl.multiple_of(first * frames, frames)
    block = rows_scr[pl.ds(start, size * frames), :].astype(BF16)
    out_ref[at : at + size] = block.reshape(size, frames, cols)


def put_anchor(out_ref, at, first, size, anchor_scr):
    _, frames, cols = out_ref.shape
    block = anchor_scr[pl.ds(pl.multiple_of(first, size), size), :].astype(BF16)
    out_ref[at : at + size // frames] = block.reshape(size // frames, frames, cols)


def put_omega(out_ref, at, omega):
    frames, cols = out_ref.shape[1], out_ref.shape[2]
    ranks = omega.shape[1]
    out_ref[at, :, 0:ranks] = omega
    out_ref[at, :, ranks:] = jnp.zeros((frames, cols - ranks), BF16)


def put_block(out_ref, at, dest, share, rows_scr, anchor_scr):
    put_rows(out_ref, at, dest * share, share, rows_scr)
    put_anchor(out_ref, at + share, dest * share, share, anchor_scr)


def put_edges(out_ref, index, rows_scr, anchor_scr, share, width, omega):
    _, frames, cols = out_ref.shape
    packed = cols // (2 * width)
    groups = share // packed
    lane = lax.broadcasted_iota(jnp.int32, (frames, cols), 1) // (2 * width)
    start = pl.multiple_of(index * (share * frames), share * frames)
    for group in range(groups):
        tile = jnp.zeros((frames, cols), F32)
        for q in range(packed):
            begin = pl.multiple_of(start + (group * packed + q) * frames, frames)
            value = rows_scr[pl.ds(begin, frames), :]
            tile = jnp.where(lane == q, turned(value, width + 2 * width * q), tile)
        out_ref[group] = tile.astype(BF16)
    first = pl.multiple_of(index * share, share)
    ranks = omega.shape[1]
    tile = jnp.concatenate([omega.astype(F32), jnp.zeros((frames, cols - ranks), F32)], axis=1)
    for q in range(2):
        at = ranks + 2 * width * q
        value = anchor_scr[pl.ds(first + q, share // 2, stride=2), :]
        if share // 2 < frames:
            value = jnp.concatenate([value, jnp.zeros((frames - share // 2, cols), F32)], axis=0)
        tile = jnp.where(lane == at // (2 * width), turned(value, width + at), tile)
    out_ref[groups] = tile.astype(BF16)


def early_kernel(axis, side, count, x_ref, taps_ref, *rest):
    outs, (a_ref, b_ref), scratch = rest[:2], rest[2:4], rest[4:]
    centre_scr, rows_scr, anchor_scr = scratch
    frames, rows, cols = x_ref.shape
    part, span = anchor_scr.shape[0], centre_scr.shape[0]
    share = part // 2
    radius = (taps_ref.shape[1] - 1) // 2
    me = lax.axis_index(axis)
    chip = device_at(me, count, count // 4, 0) // 2
    first = jnp.clip(chip * part - (span - part) // 2, 0, rows - span)
    first = pl.multiple_of(first, 16)
    inner = pl.multiple_of(chip * part - first, 16)
    taps = taps_ref[...].astype(F32)
    bx = toeplitz(taps, cols, cols, radius, -1).astype(BF16)
    dy = toeplitz(taps, part, span, radius - inner).astype(BF16)
    middle = pl.multiple_of(chip * part, part)
    total = jnp.zeros((span, cols), F32)
    for f in range(frames):
        total = total + x_ref[f, pl.ds(first, span), :].astype(F32)
    anchor = (total * (1.0 / frames)).astype(BF16)
    anchor32 = anchor.astype(F32)
    centre_scr[...] = anchor32
    centre = centre_scr[pl.ds(inner, part), :]
    blocks = [anchor]
    for f in range(frames):
        blocks.append((x_ref[f, pl.ds(first, span), :].astype(F32) - anchor32).astype(BF16))
    smooth = contract(jnp.concatenate(blocks, axis=0), bx, 1, 0)
    high, low = split(smooth[:span])
    both = contract(dy, jnp.concatenate([high, low], axis=1), 1, 0)
    anchor_s = centre - both[:, :cols] - both[:, cols:]
    anchor_out = anchor_s.astype(BF16).astype(F32)
    anchor_scr[...] = anchor_out
    left_over = anchor_s - anchor_out
    for p in range(frames // 2):
        pair = (2 * p, 2 * p + 1)
        smooths = [smooth[(f + 1) * span : (f + 2) * span].astype(BF16) for f in pair]
        both = contract(dy, jnp.concatenate(smooths, axis=1), 1, 0)
        for i, f in enumerate(pair):
            block = x_ref[f, pl.ds(middle, part), :].astype(F32) - centre
            block = block.astype(BF16).astype(F32)
            value = block - both[:, i * cols : (i + 1) * cols] + left_over
            rows_scr[pl.ds(f, part, stride=frames), :] = value
    for h, out_ref in enumerate(outs):
        put_block(out_ref, 0, (me + h) % 2, share, rows_scr, anchor_scr)

    row = lax.broadcasted_iota(jnp.int32, (2 * radius, cols), 0)
    col = lax.broadcasted_iota(jnp.int32, (2 * radius, cols), 1)
    right = (row < radius) == (lax.axis_index(side) % 2 == 0)
    wanted = row % radius + jnp.where(right, cols - radius, 0)
    pick = jnp.where(col == wanted, 1.0, 0.0).astype(BF16)
    for f in range(frames):
        both = contract(pick, x_ref[f], 1, 1).astype(BF16)
        a_ref[f] = both[:radius]
        b_ref[f] = both[radius:]


def prepare_kernel(side, x_ref, space_ref, time_ref, om_in, bh_ref, dy_ref, lhs_ref, om_ref, *rest):
    anchor_ref, block_ref, smooth_ref = rest
    om_ref[...] = om_in[...]
    frames, rows, cols = x_ref.shape
    space, time = space_ref[...].astype(F32), time_ref[...].astype(F32)
    radius = (space.shape[1] - 1) // 2
    bx = toeplitz(space, cols, cols, radius, -1).astype(BF16)
    total = jnp.zeros((rows, cols), F32)
    for f in range(frames):
        total = total + x_ref[f].astype(F32)
    anchor = (total * (1.0 / frames)).astype(BF16)
    anchor32 = anchor.astype(F32)
    anchor_ref[...] = anchor32
    smooth_ref[frames] = contract(anchor, bx, 1, 0)
    for f in range(frames):
        block = (x_ref[f].astype(F32) - anchor32).astype(BF16)
        block_ref[f] = block
        smooth_ref[f] = contract(block, bx, 1, 0)
    left = toeplitz(space, radius, cols, 0, -1)
    right = toeplitz(space, radius, cols, radius + cols, -1)
    odd = lax.axis_index(side) % 2 == 1
    bh_ref[0:radius] = jnp.where(odd, left, right).astype(BF16)
    bh_ref[radius:] = jnp.where(odd, right, left).astype(BF16)
    dy_ref[...] = toeplitz(space, rows, rows, radius).astype(BF16)
    all_frames = lhs_ref.shape[0]
    count = (lhs_ref.shape[1] - all_frames) // 2
    frames = all_frames // count
    band = toeplitz(time, all_frames, all_frames, radius)
    ids = lax.broadcasted_iota(jnp.int32, (all_frames, count), 0) // frames
    lane = lax.broadcasted_iota(jnp.int32, (all_frames, count), 1)
    sums = jnp.where(ids == lane, 1.0, 0.0)
    for j in range(count):
        piece = jnp.sum(band[:, j * frames : (j + 1) * frames], axis=1, keepdims=True)
        sums = jnp.where(lane == j, sums - piece, sums)
    high, low = split(sums)
    lhs_ref[:, 0:all_frames] = (-band).astype(BF16)
    lhs_ref[:, all_frames:] = jnp.concatenate([high.astype(F32), low.astype(F32)], 1).astype(BF16)


def spatial_kernel(axis, a_ref, b_ref, bh_ref, dy_ref, om_ref, *rest):
    (anchor_ref, block_ref, smooth_ref), rest = rest[:3], rest[3:]
    outs, edge_refs, (rows_scr, anchor_scr, smooth_scr) = rest[:-5], rest[-5:-3], rest[-3:]
    frames, rows, cols = block_ref.shape
    radius = a_ref.shape[1]
    share = (outs[0].shape[0] - 1) * frames // (frames + 1)
    count = rows // share
    me = lax.axis_index(axis)
    bh, dy = bh_ref[...], dy_ref[...]

    def halo(f):
        return jnp.concatenate([a_ref[f].astype(F32), b_ref[f].astype(F32)], axis=0)

    def across(f, edge):
        return smooth_ref[f] + contract(edge, bh, 0, 0)

    total = halo(0)
    for f in range(1, frames):
        total = total + halo(f)
    edge_anchor = (total * (1.0 / frames)).astype(BF16)
    edge32 = edge_anchor.astype(F32)
    for f in range(frames):
        smooth_scr[f] = across(f, (halo(f) - edge32).astype(BF16)).astype(BF16)
    high, low = split(across(frames, edge_anchor))
    both = contract(dy, jnp.concatenate([high, low], axis=1), 1, 0)
    anchor_s = anchor_ref[...] - both[:, :cols] - both[:, cols:]
    anchor_out = anchor_s.astype(BF16).astype(F32)
    anchor_scr[...] = anchor_out
    left_over = anchor_s - anchor_out
    for p in range(frames // 2):
        pair = (2 * p, 2 * p + 1)
        both = contract(dy, jnp.concatenate([smooth_scr[f] for f in pair], axis=1), 1, 0)
        for i, f in enumerate(pair):
            value = block_ref[f].astype(F32) - both[:, i * cols : (i + 1) * cols] + left_over
            rows_scr[pl.ds(f, rows, stride=frames), :] = value
    early = count // 4
    for (shift, flips), out in zip(message_list(count), outs):
        for i, flip in enumerate(flips):
            dest = device_at(me, count, shift, flip)
            at = i * (share + share // frames + 1)
            put_block(out, at, dest, share, rows_scr, anchor_scr)
            put_omega(out, at + share + share // frames, om_ref[dest // (count // TY)])
    for h, out in enumerate(edge_refs):
        dest = device_at(me, count, early, h)
        omega = om_ref[dest // (count // TY)]
        put_edges(out, dest, rows_scr, anchor_scr, share, radius, omega)


def message_list(count):
    return [(c, (flip,)) for c in range(count // 2) if c != count // 4 for flip in range(2)]


def take_block(data_ref, anchor_ref, ref, at, src):
    share, count, frames, cols = data_ref.shape
    data_ref[:, src] = ref[at : at + share]
    anchor = ref[at + share : at + share + share // frames].reshape(share, cols)
    anchor_ref[pl.ds(src, share, stride=count), :] = anchor.astype(F32)


def take_edges(data_ref, anchor_ref, ref, src, width, ranks):
    share, count, frames, cols = data_ref.shape
    packed = cols // (2 * width)
    groups = share // packed
    lanes = lax.broadcasted_iota(jnp.int32, (frames, cols), 1)
    at_edge = (lanes < width) | (lanes >= cols - width)
    last = ref[groups].astype(F32)
    for q in range(2):
        edge = turned(last, -(width + ranks + 2 * width * q))[: share // 2]
        where = pl.ds(src + q * count, share // 2, stride=2 * count)
        old = anchor_ref[where, :]
        anchor_ref[where, :] = jnp.where(at_edge[: share // 2], edge, old)
    for group in range(groups):
        tile = ref[group].astype(F32)
        for q in range(packed):
            r = group * packed + q
            edge = turned(tile, -(width + 2 * width * q))
            value = jnp.where(at_edge, edge, data_ref[r, src].astype(F32))
            data_ref[r, src] = value.astype(BF16)


def gather_kernel(axis, places, *refs):
    blocks, mains, (data_ref, anchor_ref, om_ref) = refs[:-5], refs[-5:-3], refs[-3:]
    share, count, frames, _ = data_ref.shape
    slots = share + share // frames
    me = lax.axis_index(axis)
    for (shift, flip), ref in zip(places, blocks):
        src = device_at(me, count, -shift, flip)
        take_block(data_ref, anchor_ref, ref, 0, src)
        om_ref[src] = ref[slots]
    for h, ref in enumerate(mains):
        take_block(data_ref, anchor_ref, ref, 0, device_at(me, count, -(count // 4), h))


def temporal_kernel(axis, width, ranks, places, *refs):
    blocks, edge_refs, lhs_ref = refs[3:-9], refs[-9:-7], refs[-7]
    data_ref, anchor_ref, om_ref, m_ref, gram_ref, turned_ref = refs[-6:]
    share, count, frames, cols = data_ref.shape
    all_frames = count * frames
    slots = share + share // frames
    me = lax.axis_index(axis)
    for (shift, flip), ref in zip(places, blocks):
        src = device_at(me, count, -shift, flip)
        take_block(data_ref, anchor_ref, ref, 0, src)
        om_ref[src] = ref[slots]
    for h, ref in enumerate(edge_refs):
        src = device_at(me, count, -(count // 4), h)
        take_edges(data_ref, anchor_ref, ref, src, width, ranks)
        om_ref[src] = ref[ref.shape[0] - 1]
    lhs = lhs_ref[...]
    gram = jnp.zeros((all_frames, all_frames), F32)
    for p in range(share // 2):
        blocks, feeds = [], []
        for r in (2 * p, 2 * p + 1):
            block = data_ref[r].reshape(all_frames, cols)
            anchor = anchor_ref[r * count : (r + 1) * count, :]
            blocks.append(block)
            feeds.append(
                jnp.concatenate([block, jnp.concatenate([anchor, anchor], 0).astype(BF16)], axis=0)
            )
        low = contract(lhs, jnp.concatenate(feeds, axis=1), 1, 0)
        value = (jnp.concatenate(blocks, axis=1).astype(F32) + low).astype(BF16)
        m_ref[2 * p] = value[:, :cols]
        m_ref[2 * p + 1] = value[:, cols:]
        gram = gram + contract(value, value, 1, 1)
    gram_ref[...] = gram
    omega = om_ref[...].reshape(all_frames, cols).astype(F32)
    turned_ref[...] = omega.T[:ranks]


def exact(left, right, left_dim, right_dim):
    return lax.dot_general(
        left,
        right,
        (((left_dim,), (right_dim,)), ((), ())),
        precision=lax.Precision.HIGHEST,
        preferred_element_type=F32,
    )


def whiten(gram, *others):
    size = gram.shape[0]
    ids = lax.broadcasted_iota(jnp.int32, (size, 128), 0)
    work = [jnp.concatenate([gram, jnp.zeros((size, 128 - size), F32)], axis=1), *others]
    scale = jnp.zeros((size, 128), F32)
    panel = 16
    for start in range(0, size, panel):
        cols = [
            jnp.broadcast_to(work[0][:, j : j + 1], (size, 128)) for j in range(start, start + panel)
        ]
        for j in range(start, start + panel):
            inverse = 1.0 / cols[j - start][j : j + 1]
            factor = jnp.where(ids > j, cols[j - start], 0.0) * inverse
            scale = jnp.where(ids == j, inverse, scale)
            for m in range(j - start + 1, panel):
                cols[m] = cols[m] - factor * cols[m][j : j + 1]
            for i in range(len(work)):
                value = work[i]
                width = value.shape[1]
                parts = [
                    value[:, c : c + 128] - factor * value[j : j + 1, c : c + 128]
                    for c in range(0, width, 128)
                ]
                work[i] = parts[0] if len(parts) == 1 else jnp.concatenate(parts, axis=1)
    scale = jnp.sqrt(scale)
    results = []
    for value in work[1:]:
        parts = [value[:, c : c + 128] * scale for c in range(0, value.shape[1], 128)]
        results.append(parts[0] if len(parts) == 1 else jnp.concatenate(parts, axis=1))
    return results


def factor_kernel(axis, count, ranks, pixels, om_ref, *refs):
    grams, (mix_ref, own_ref, send_ref, coef_scr) = refs[:-4], refs[-4:]
    frames = own_ref.shape[1]
    all_frames = grams[0].shape[0]
    me = lax.axis_index(axis)
    gram = grams[0][...]
    for other in grams[1:]:
        gram = gram + other[...]
    omega = om_ref[...]
    sketch = exact(omega, gram, 1, 0)
    (load,) = whiten(exact(sketch, omega, 1, 1), sketch)
    back = exact(load, gram, 1, 0)
    mix, coef = whiten(exact(back, load, 1, 1), load, back)
    mix_ref[...] = mix * math.sqrt(pixels)
    coef_scr[...] = coef.T
    for ref, who in ((own_ref, me), (send_ref, me ^ (count // TY))):
        ref[...] = jnp.zeros_like(ref)
        start = pl.multiple_of(who * frames, frames)
        ref[me // (count // TY)] = coef_scr[pl.ds(start, frames), :]


def basis_kernel(m_ref, mix_ref, out_ref):
    share, _, cols = m_ref.shape
    ranks = mix_ref.shape[0]
    high, low = split(mix_ref[...])
    lhs = jnp.concatenate([high, low], axis=0)
    for p in range(share // 2):
        data = jnp.concatenate([m_ref[2 * p], m_ref[2 * p + 1]], axis=1)
        both = contract(lhs, data, 1, 0)
        value = both[:ranks] + both[ranks:]
        for i in range(2):
            out_ref[pl.ds(2 * p + i, ranks, stride=share), :] = value[:, i * cols : (i + 1) * cols]


def local(movie, omega, time_taps, space_taps):
    frames, rows, cols = movie.shape
    radius = (space_taps.shape[0] - 1) // 2
    count = lax.axis_size("tm")
    tiles = lax.axis_size("tile")
    ranks = omega.shape[2]
    share = rows // count
    all_frames = frames * count
    group = count // TY
    pixels = (rows // TY) * cols
    early = count // 4
    packed = cols // (2 * radius)
    slots = share + share // frames

    def shape(dims, dtype):
        return jax.ShapeDtypeStruct(dims, dtype)

    def swap(value, k):
        return lax.ppermute(value, "tm", [(i, i ^ k) for i in range(count)])

    def send(value, shift, flip):
        return lax.ppermute(value, "tm", [(i, device_at(i, count, shift, flip)) for i in range(count)])

    space_row, time_row = space_taps.astype(F32)[None], time_taps[None]
    part = 2 * share
    span = part + 32
    *mains, side_a, side_b = call(
        functools.partial(early_kernel, "tm", "tile", count),
        [
            *([shape((slots, frames, cols), BF16)] * 2),
            *([shape((frames, radius, rows), BF16)] * 2),
        ],
        [movie, space_row],
        [
            pltpu.VMEM((span, cols), F32),
            pltpu.VMEM((part * frames, cols), F32),
            pltpu.VMEM((part, cols), F32),
        ],
    )
    mains = [send(value, early, h) for h, value in enumerate(mains)]
    pairs = [(i, i ^ 1) for i in range(tiles)]
    side_a = lax.ppermute(side_a, "tile", pairs)
    pairs = [(i, i + 1) for i in range(1, tiles - 1, 2)]
    side_b = lax.ppermute(side_b, "tile", pairs + [(j, i) for i, j in pairs])
    om = jnp.transpose(omega[:, 0], (0, 2, 1))
    bh, dy, lhs, om, *prepared = call(
        functools.partial(prepare_kernel, "tile"),
        [
            shape((2 * radius, cols), BF16),
            shape((rows, rows), BF16),
            shape((all_frames, all_frames + 2 * count), BF16),
            shape(om.shape, om.dtype),
            shape((rows, cols), F32),
            shape(movie.shape, BF16),
            shape((frames + 1, rows, cols), F32),
        ],
        [movie, space_row, time_row, om],
    )
    listed = message_list(count)
    *parts, edges, edges_other = call(
        functools.partial(spatial_kernel, "tm"),
        [
            *[shape((len(flips) * (slots + 1), frames, cols), BF16) for _, flips in listed],
            *([shape((share // packed + 1, frames, cols), BF16)] * 2),
        ],
        [side_a, side_b, bh, dy, om, *prepared],
        [
            pltpu.VMEM((rows * frames, cols), F32),
            pltpu.VMEM((rows, cols), F32),
            pltpu.VMEM(movie.shape, BF16),
        ],
    )
    def after(value, *others):
        return lax.optimization_barrier((value, *others))[0]

    parts[-1] = after(parts[-1], *mains)
    blocks = [parts[0]] + [
        send(value, shift, flip) for (shift, (flip,)), value in zip(listed[1:], parts[1:])
    ]
    edges = send(after(edges, blocks[1]), early, 0)
    edges_other = send(after(edges_other, blocks[1]), early, 1)
    places = [(shift, flip) for shift, flips in listed for flip in flips]
    known = call(
        functools.partial(gather_kernel, "tm", places[:-2]),
        [
            shape((share, count, frames, cols), BF16),
            shape((share * count, cols), F32),
            shape((count, frames, cols), BF16),
        ],
        [*blocks[:-2], *mains],
    )
    *_, matrix, gram, om_all = call(
        functools.partial(temporal_kernel, "tm", radius, ranks, places[-2:]),
        [
            *[shape(value.shape, value.dtype) for value in known],
            shape((share, all_frames, cols), BF16),
            shape((all_frames, all_frames), F32),
            shape((ranks, all_frames), F32),
        ],
        [*known, *blocks[-2:], edges, edges_other, lhs],
        aliases={0: 0, 1: 1, 2: 2},
    )
    chips = [gram] + [swap(gram, k) for k in range(2, group, 2)]
    grams = chips + [swap(value, 1) for value in chips]
    mix, coef_own, coef_send = call(
        functools.partial(factor_kernel, "tm", count, ranks, pixels),
        [shape((ranks, all_frames), F32), *([shape((TY, frames, ranks), F32)] * 2)],
        [om_all, *grams],
        [pltpu.VMEM((all_frames, ranks), F32)],
    )
    coef_other = swap(coef_send, group)
    (basis,) = call(basis_kernel, [shape((ranks * share, cols), F32)], [matrix, mix])
    coefficients = jnp.transpose(coef_own + coef_other, (0, 2, 1))[:, None]
    return basis.reshape(ranks, share, cols), coefficients


def solution(mesh):
    in_specs = (P("tm", None, "tile"), P(None, "tile", None, "tm"), P(), P())
    out_specs = (P(None, "tm", "tile"), P(None, "tile", None, "tm"))
    return jax.shard_map(local, mesh=mesh, in_specs=in_specs, out_specs=out_specs, check_vma=False)
```

```python
import functools
import math

import jax
import jax.numpy as jnp
from jax import lax
from jax.experimental import pallas as pl
from jax.experimental.pallas import tpu as pltpu
from jax.sharding import PartitionSpec as P

TY = 2
F32 = jnp.float32
BF16 = jnp.bfloat16


def call(kernel, outs, ins, scratch=(), places=None, grant=40 << 20, aliases=None):
    places = places or [pltpu.VMEM] * len(ins)
    return pl.pallas_call(
        kernel,
        out_shape=outs,
        in_specs=[pl.BlockSpec(memory_space=place) for place in places],
        out_specs=[pl.BlockSpec(memory_space=pltpu.VMEM)] * len(outs),
        scratch_shapes=scratch,
        input_output_aliases=aliases or {},
        compiler_params=pltpu.CompilerParams(vmem_limit_bytes=grant),
        cost_estimate=pl.CostEstimate(flops=0, bytes_accessed=0, transcendentals=0),
    )(*ins)


def toeplitz(tap_row, rows, cols, shift, sign=1):
    offsets = sign * (
        lax.broadcasted_iota(jnp.int32, (rows, cols), 1)
        - lax.broadcasted_iota(jnp.int32, (rows, cols), 0)
    )
    offsets = offsets + shift
    total = jnp.zeros((rows, cols), F32)
    for t in range(tap_row.shape[1]):
        total = jnp.where(offsets == t, tap_row[:, t : t + 1], total)
    return total


def contract(left, right, left_dim, right_dim):
    return lax.dot_general(
        left, right, (((left_dim,), (right_dim,)), ((), ())), preferred_element_type=F32
    )


def split(value):
    high = value.astype(BF16)
    return high, (value - high.astype(F32)).astype(BF16)


def turned(value, shift):
    return pltpu.roll(value, shift % value.shape[1], 1)


def device_at(index, count, shift, flip):
    return (index // 2 + shift) % (count // 2) * 2 + (index % 2 + flip) % 2


def put_rows(out_ref, at, first, size, rows_scr):
    _, frames, cols = out_ref.shape
    start = pl.multiple_of(first * frames, frames)
    block = rows_scr[pl.ds(start, size * frames), :].astype(BF16)
    out_ref[at : at + size] = block.reshape(size, frames, cols)


def put_anchor(out_ref, at, first, size, anchor_scr):
    _, frames, cols = out_ref.shape
    block = anchor_scr[pl.ds(pl.multiple_of(first, size), size), :].astype(BF16)
    out_ref[at : at + size // frames] = block.reshape(size // frames, frames, cols)


def put_omega(out_ref, at, omega):
    frames, cols = out_ref.shape[1], out_ref.shape[2]
    ranks = omega.shape[1]
    out_ref[at, :, 0:ranks] = omega
    out_ref[at, :, ranks:] = jnp.zeros((frames, cols - ranks), BF16)


def put_block(out_ref, at, dest, share, rows_scr, anchor_scr):
    put_rows(out_ref, at, dest * share, share, rows_scr)
    put_anchor(out_ref, at + share, dest * share, share, anchor_scr)


def put_edges(out_ref, index, rows_scr, anchor_scr, share, width, omega):
    _, frames, cols = out_ref.shape
    packed = cols // (2 * width)
    groups = share // packed
    lane = lax.broadcasted_iota(jnp.int32, (frames, cols), 1) // (2 * width)
    start = pl.multiple_of(index * (share * frames), share * frames)
    for group in range(groups):
        tile = jnp.zeros((frames, cols), F32)
        for q in range(packed):
            begin = pl.multiple_of(start + (group * packed + q) * frames, frames)
            value = rows_scr[pl.ds(begin, frames), :]
            tile = jnp.where(lane == q, turned(value, width + 2 * width * q), tile)
        out_ref[group] = tile.astype(BF16)
    first = pl.multiple_of(index * share, share)
    ranks = omega.shape[1]
    tile = jnp.concatenate([omega.astype(F32), jnp.zeros((frames, cols - ranks), F32)], axis=1)
    for q in range(2):
        at = ranks + 2 * width * q
        value = anchor_scr[pl.ds(first + q, share // 2, stride=2), :]
        if share // 2 < frames:
            value = jnp.concatenate([value, jnp.zeros((frames - share // 2, cols), F32)], axis=0)
        tile = jnp.where(lane == at // (2 * width), turned(value, width + at), tile)
    out_ref[groups] = tile.astype(BF16)


def early_kernel(axis, side, count, x_ref, taps_ref, *rest):
    outs, (a_ref, b_ref), scratch = rest[:2], rest[2:4], rest[4:]
    centre_scr, rows_scr, anchor_scr = scratch
    frames, rows, cols = x_ref.shape
    part, span = anchor_scr.shape[0], centre_scr.shape[0]
    share = part // 2
    radius = (taps_ref.shape[1] - 1) // 2
    me = lax.axis_index(axis)
    chip = device_at(me, count, count // 4, 0) // 2
    first = jnp.clip(chip * part - (span - part) // 2, 0, rows - span)
    first = pl.multiple_of(first, 16)
    inner = pl.multiple_of(chip * part - first, 16)
    taps = taps_ref[...].astype(F32)
    bx = toeplitz(taps, cols, cols, radius, -1).astype(BF16)
    dy = toeplitz(taps, part, span, radius - inner).astype(BF16)
    middle = pl.multiple_of(chip * part, part)
    total = jnp.zeros((span, cols), F32)
    for f in range(frames):
        total = total + x_ref[f, pl.ds(first, span), :].astype(F32)
    anchor = (total * (1.0 / frames)).astype(BF16)
    anchor32 = anchor.astype(F32)
    centre_scr[...] = anchor32
    centre = centre_scr[pl.ds(inner, part), :]
    blocks = [anchor]
    for f in range(frames):
        blocks.append((x_ref[f, pl.ds(first, span), :].astype(F32) - anchor32).astype(BF16))
    smooth = contract(jnp.concatenate(blocks, axis=0), bx, 1, 0)
    high, low = split(smooth[:span])
    both = contract(dy, jnp.concatenate([high, low], axis=1), 1, 0)
    anchor_s = centre - both[:, :cols] - both[:, cols:]
    anchor_out = anchor_s.astype(BF16).astype(F32)
    anchor_scr[...] = anchor_out
    left_over = anchor_s - anchor_out
    for p in range(frames // 2):
        pair = (2 * p, 2 * p + 1)
        smooths = [smooth[(f + 1) * span : (f + 2) * span].astype(BF16) for f in pair]
        both = contract(dy, jnp.concatenate(smooths, axis=1), 1, 0)
        for i, f in enumerate(pair):
            block = x_ref[f, pl.ds(middle, part), :].astype(F32) - centre
            block = block.astype(BF16).astype(F32)
            value = block - both[:, i * cols : (i + 1) * cols] + left_over
            rows_scr[pl.ds(f, part, stride=frames), :] = value
    for h, out_ref in enumerate(outs):
        put_block(out_ref, 0, (me + h) % 2, share, rows_scr, anchor_scr)

    row = lax.broadcasted_iota(jnp.int32, (2 * radius, cols), 0)
    col = lax.broadcasted_iota(jnp.int32, (2 * radius, cols), 1)
    right = (row < radius) == (lax.axis_index(side) % 2 == 0)
    wanted = row % radius + jnp.where(right, cols - radius, 0)
    pick = jnp.where(col == wanted, 1.0, 0.0).astype(BF16)
    for f in range(frames):
        both = contract(pick, x_ref[f], 1, 1).astype(BF16)
        a_ref[f] = both[:radius]
        b_ref[f] = both[radius:]


def prepare_kernel(side, x_ref, space_ref, time_ref, om_in, bh_ref, dy_ref, lhs_ref, om_ref, *rest):
    anchor_ref, block_ref, smooth_ref = rest
    om_ref[...] = om_in[...]
    frames, rows, cols = x_ref.shape
    space, time = space_ref[...].astype(F32), time_ref[...].astype(F32)
    radius = (space.shape[1] - 1) // 2
    bx = toeplitz(space, cols, cols, radius, -1).astype(BF16)
    total = jnp.zeros((rows, cols), F32)
    for f in range(frames):
        total = total + x_ref[f].astype(F32)
    anchor = (total * (1.0 / frames)).astype(BF16)
    anchor32 = anchor.astype(F32)
    anchor_ref[...] = anchor32
    smooth_ref[frames] = contract(anchor, bx, 1, 0)
    for f in range(frames):
        block = (x_ref[f].astype(F32) - anchor32).astype(BF16)
        block_ref[f] = block
        smooth_ref[f] = contract(block, bx, 1, 0)
    left = toeplitz(space, radius, cols, 0, -1)
    right = toeplitz(space, radius, cols, radius + cols, -1)
    odd = lax.axis_index(side) % 2 == 1
    bh_ref[0:radius] = jnp.where(odd, left, right).astype(BF16)
    bh_ref[radius:] = jnp.where(odd, right, left).astype(BF16)
    dy_ref[...] = toeplitz(space, rows, rows, radius).astype(BF16)
    all_frames = lhs_ref.shape[0]
    count = (lhs_ref.shape[1] - all_frames) // 2
    frames = all_frames // count
    band = toeplitz(time, all_frames, all_frames, radius)
    ids = lax.broadcasted_iota(jnp.int32, (all_frames, count), 0) // frames
    lane = lax.broadcasted_iota(jnp.int32, (all_frames, count), 1)
    sums = jnp.where(ids == lane, 1.0, 0.0)
    for j in range(count):
        piece = jnp.sum(band[:, j * frames : (j + 1) * frames], axis=1, keepdims=True)
        sums = jnp.where(lane == j, sums - piece, sums)
    high, low = split(sums)
    lhs_ref[:, 0:all_frames] = (-band).astype(BF16)
    lhs_ref[:, all_frames:] = jnp.concatenate([high.astype(F32), low.astype(F32)], 1).astype(BF16)


def spatial_kernel(axis, a_ref, b_ref, bh_ref, dy_ref, om_ref, *rest):
    (anchor_ref, block_ref, smooth_ref), rest = rest[:3], rest[3:]
    outs, edge_refs, (rows_scr, anchor_scr) = rest[:-4], rest[-4:-2], rest[-2:]
    frames, rows, cols = block_ref.shape
    radius = a_ref.shape[1]
    share = (outs[0].shape[0] - 1) * frames // (frames + 1)
    count = rows // share
    me = lax.axis_index(axis)
    bh, dy = bh_ref[...], dy_ref[...]

    def halo(f):
        return jnp.concatenate([a_ref[f].astype(F32), b_ref[f].astype(F32)], axis=0)

    def across(f, edge):
        return smooth_ref[f] + contract(edge, bh, 0, 0)

    total = halo(0)
    for f in range(1, frames):
        total = total + halo(f)
    edge_anchor = (total * (1.0 / frames)).astype(BF16)
    edge32 = edge_anchor.astype(F32)
    high, low = split(across(frames, edge_anchor))
    both = contract(dy, jnp.concatenate([high, low], axis=1), 1, 0)
    anchor_s = anchor_ref[...] - both[:, :cols] - both[:, cols:]
    anchor_out = anchor_s.astype(BF16).astype(F32)
    anchor_scr[...] = anchor_out
    left_over = anchor_s - anchor_out
    for p in range(frames // 2):
        pair = (2 * p, 2 * p + 1)
        smooths = [across(f, (halo(f) - edge32).astype(BF16)).astype(BF16) for f in pair]
        both = contract(dy, jnp.concatenate(smooths, axis=1), 1, 0)
        for i, f in enumerate(pair):
            value = block_ref[f].astype(F32) - both[:, i * cols : (i + 1) * cols] + left_over
            rows_scr[pl.ds(f, rows, stride=frames), :] = value
    early = count // 4
    for (shift, flips), out in zip(message_list(count), outs):
        for i, flip in enumerate(flips):
            dest = device_at(me, count, shift, flip)
            at = i * (share + share // frames + 1)
            put_block(out, at, dest, share, rows_scr, anchor_scr)
            put_omega(out, at + share + share // frames, om_ref[dest // (count // TY)])
    for h, out in enumerate(edge_refs):
        dest = device_at(me, count, early, h)
        omega = om_ref[dest // (count // TY)]
        put_edges(out, dest, rows_scr, anchor_scr, share, radius, omega)


def message_list(count):
    return [(c, (flip,)) for c in range(count // 2) if c != count // 4 for flip in range(2)]


def take_block(data_ref, anchor_ref, ref, at, src):
    share, count, frames, cols = data_ref.shape
    data_ref[:, src] = ref[at : at + share]
    anchor = ref[at + share : at + share + share // frames].reshape(share, cols)
    anchor_ref[pl.ds(src, share, stride=count), :] = anchor.astype(F32)


def take_edges(data_ref, anchor_ref, ref, src, width, ranks):
    share, count, frames, cols = data_ref.shape
    packed = cols // (2 * width)
    groups = share // packed
    lanes = lax.broadcasted_iota(jnp.int32, (frames, cols), 1)
    at_edge = (lanes < width) | (lanes >= cols - width)
    last = ref[groups].astype(F32)
    for q in range(2):
        edge = turned(last, -(width + ranks + 2 * width * q))[: share // 2]
        where = pl.ds(src + q * count, share // 2, stride=2 * count)
        old = anchor_ref[where, :]
        anchor_ref[where, :] = jnp.where(at_edge[: share // 2], edge, old)
    for group in range(groups):
        tile = ref[group].astype(F32)
        for q in range(packed):
            r = group * packed + q
            edge = turned(tile, -(width + 2 * width * q))
            value = jnp.where(at_edge, edge, data_ref[r, src].astype(F32))
            data_ref[r, src] = value.astype(BF16)


def gather_kernel(axis, places, *refs):
    blocks, mains, (data_ref, anchor_ref, om_ref) = refs[:-5], refs[-5:-3], refs[-3:]
    share, count, frames, _ = data_ref.shape
    slots = share + share // frames
    me = lax.axis_index(axis)
    for (shift, flip), ref in zip(places, blocks):
        src = device_at(me, count, -shift, flip)
        take_block(data_ref, anchor_ref, ref, 0, src)
        om_ref[src] = ref[slots]
    for h, ref in enumerate(mains):
        take_block(data_ref, anchor_ref, ref, 0, device_at(me, count, -(count // 4), h))


def temporal_kernel(axis, width, ranks, places, *refs):
    blocks, edge_refs, lhs_ref = refs[3:-9], refs[-9:-7], refs[-7]
    data_ref, anchor_ref, om_ref, m_ref, gram_ref, turned_ref = refs[-6:]
    share, count, frames, cols = data_ref.shape
    all_frames = count * frames
    slots = share + share // frames
    me = lax.axis_index(axis)
    for (shift, flip), ref in zip(places, blocks):
        src = device_at(me, count, -shift, flip)
        take_block(data_ref, anchor_ref, ref, 0, src)
        om_ref[src] = ref[slots]
    for h, ref in enumerate(edge_refs):
        src = device_at(me, count, -(count // 4), h)
        take_edges(data_ref, anchor_ref, ref, src, width, ranks)
        om_ref[src] = ref[ref.shape[0] - 1]
    lhs = lhs_ref[...]
    gram = jnp.zeros((all_frames, all_frames), F32)
    for p in range(share // 2):
        blocks, feeds = [], []
        for r in (2 * p, 2 * p + 1):
            block = data_ref[r].reshape(all_frames, cols)
            anchor = anchor_ref[r * count : (r + 1) * count, :]
            blocks.append(block)
            feeds.append(
                jnp.concatenate([block, jnp.concatenate([anchor, anchor], 0).astype(BF16)], axis=0)
            )
        low = contract(lhs, jnp.concatenate(feeds, axis=1), 1, 0)
        value = (jnp.concatenate(blocks, axis=1).astype(F32) + low).astype(BF16)
        m_ref[2 * p] = value[:, :cols]
        m_ref[2 * p + 1] = value[:, cols:]
        gram = gram + contract(value, value, 1, 1)
    gram_ref[...] = gram
    omega = om_ref[...].reshape(all_frames, cols).astype(F32)
    turned_ref[...] = omega.T[:ranks]


def exact(left, right, left_dim, right_dim):
    return lax.dot_general(
        left,
        right,
        (((left_dim,), (right_dim,)), ((), ())),
        precision=lax.Precision.HIGHEST,
        preferred_element_type=F32,
    )


def whiten(gram, *others):
    size = gram.shape[0]
    ids = lax.broadcasted_iota(jnp.int32, (size, 128), 0)
    work = [jnp.concatenate([gram, jnp.zeros((size, 128 - size), F32)], axis=1), *others]
    scale = jnp.zeros((size, 128), F32)
    panel = 16
    for start in range(0, size, panel):
        cols = [
            jnp.broadcast_to(work[0][:, j : j + 1], (size, 128)) for j in range(start, start + panel)
        ]
        for j in range(start, start + panel):
            inverse = 1.0 / cols[j - start][j : j + 1]
            factor = jnp.where(ids > j, cols[j - start], 0.0) * inverse
            scale = jnp.where(ids == j, inverse, scale)
            for m in range(j - start + 1, panel):
                cols[m] = cols[m] - factor * cols[m][j : j + 1]
            for i in range(len(work)):
                value = work[i]
                width = value.shape[1]
                parts = [
                    value[:, c : c + 128] - factor * value[j : j + 1, c : c + 128]
                    for c in range(0, width, 128)
                ]
                work[i] = parts[0] if len(parts) == 1 else jnp.concatenate(parts, axis=1)
    scale = jnp.sqrt(scale)
    results = []
    for value in work[1:]:
        parts = [value[:, c : c + 128] * scale for c in range(0, value.shape[1], 128)]
        results.append(parts[0] if len(parts) == 1 else jnp.concatenate(parts, axis=1))
    return results


def factor_kernel(axis, count, ranks, pixels, om_ref, *refs):
    grams, (mix_ref, own_ref, send_ref, coef_scr) = refs[:-4], refs[-4:]
    frames = own_ref.shape[1]
    all_frames = grams[0].shape[0]
    me = lax.axis_index(axis)
    gram = grams[0][...]
    for other in grams[1:]:
        gram = gram + other[...]
    omega = om_ref[...]
    sketch = exact(omega, gram, 1, 0)
    (load,) = whiten(exact(sketch, omega, 1, 1), sketch)
    back = exact(load, gram, 1, 0)
    mix, coef = whiten(exact(back, load, 1, 1), load, back)
    mix_ref[...] = mix * math.sqrt(pixels)
    coef_scr[...] = coef.T
    for ref, who in ((own_ref, me), (send_ref, me ^ (count // TY))):
        ref[...] = jnp.zeros_like(ref)
        start = pl.multiple_of(who * frames, frames)
        ref[me // (count // TY)] = coef_scr[pl.ds(start, frames), :]


def basis_kernel(m_ref, mix_ref, out_ref):
    share, _, cols = m_ref.shape
    ranks = mix_ref.shape[0]
    high, low = split(mix_ref[...])
    lhs = jnp.concatenate([high, low], axis=0)
    for p in range(share // 2):
        data = jnp.concatenate([m_ref[2 * p], m_ref[2 * p + 1]], axis=1)
        both = contract(lhs, data, 1, 0)
        value = both[:ranks] + both[ranks:]
        for i in range(2):
            out_ref[pl.ds(2 * p + i, ranks, stride=share), :] = value[:, i * cols : (i + 1) * cols]


def local(movie, omega, time_taps, space_taps):
    frames, rows, cols = movie.shape
    radius = (space_taps.shape[0] - 1) // 2
    count = lax.axis_size("tm")
    tiles = lax.axis_size("tile")
    ranks = omega.shape[2]
    share = rows // count
    all_frames = frames * count
    group = count // TY
    pixels = (rows // TY) * cols
    early = count // 4
    packed = cols // (2 * radius)
    slots = share + share // frames

    def shape(dims, dtype):
        return jax.ShapeDtypeStruct(dims, dtype)

    def swap(value, k):
        return lax.ppermute(value, "tm", [(i, i ^ k) for i in range(count)])

    def send(value, shift, flip):
        return lax.ppermute(value, "tm", [(i, device_at(i, count, shift, flip)) for i in range(count)])

    space_row, time_row = space_taps[None], time_taps[None]
    part = 2 * share
    span = part + 32
    *mains, side_a, side_b = call(
        functools.partial(early_kernel, "tm", "tile", count),
        [
            *([shape((slots, frames, cols), BF16)] * 2),
            *([shape((frames, radius, rows), BF16)] * 2),
        ],
        [movie, space_row],
        [
            pltpu.VMEM((span, cols), F32),
            pltpu.VMEM((part * frames, cols), F32),
            pltpu.VMEM((part, cols), F32),
        ],
    )
    mains = [send(value, early, h) for h, value in enumerate(mains)]
    pairs = [(i, i ^ 1) for i in range(tiles)]
    side_a = lax.ppermute(side_a, "tile", pairs)
    pairs = [(i, i + 1) for i in range(1, tiles - 1, 2)]
    side_b = lax.ppermute(side_b, "tile", pairs + [(j, i) for i, j in pairs])
    om = jnp.transpose(omega[:, 0], (0, 2, 1))
    bh, dy, lhs, om, *prepared = call(
        functools.partial(prepare_kernel, "tile"),
        [
            shape((2 * radius, cols), BF16),
            shape((rows, rows), BF16),
            shape((all_frames, all_frames + 2 * count), BF16),
            shape(om.shape, om.dtype),
            shape((rows, cols), F32),
            shape(movie.shape, BF16),
            shape((frames + 1, rows, cols), F32),
        ],
        [movie, space_row, time_row, om],
    )
    listed = message_list(count)
    *parts, edges, edges_other = call(
        functools.partial(spatial_kernel, "tm"),
        [
            *[shape((len(flips) * (slots + 1), frames, cols), BF16) for _, flips in listed],
            *([shape((share // packed + 1, frames, cols), BF16)] * 2),
        ],
        [side_a, side_b, bh, dy, om, *prepared],
        [pltpu.VMEM((rows * frames, cols), F32), pltpu.VMEM((rows, cols), F32)],
    )
    def after(value, *others):
        return lax.optimization_barrier((value, *others))[0]

    parts[-1] = after(parts[-1], *mains)
    blocks = [parts[0]] + [
        send(value, shift, flip) for (shift, (flip,)), value in zip(listed[1:], parts[1:])
    ]
    edges = send(after(edges, blocks[1]), early, 0)
    edges_other = send(after(edges_other, blocks[1]), early, 1)
    places = [(shift, flip) for shift, flips in listed for flip in flips]
    known = call(
        functools.partial(gather_kernel, "tm", places[:-2]),
        [
            shape((share, count, frames, cols), BF16),
            shape((share * count, cols), F32),
            shape((count, frames, cols), BF16),
        ],
        [*blocks[:-2], *mains],
    )
    *_, matrix, gram, om_all = call(
        functools.partial(temporal_kernel, "tm", radius, ranks, places[-2:]),
        [
            *[shape(value.shape, value.dtype) for value in known],
            shape((share, all_frames, cols), BF16),
            shape((all_frames, all_frames), F32),
            shape((ranks, all_frames), F32),
        ],
        [*known, *blocks[-2:], edges, edges_other, lhs],
        aliases={0: 0, 1: 1, 2: 2},
    )
    chips = [gram] + [swap(gram, k) for k in range(2, group, 2)]
    grams = chips + [swap(value, 1) for value in chips]
    mix, coef_own, coef_send = call(
        functools.partial(factor_kernel, "tm", count, ranks, pixels),
        [shape((ranks, all_frames), F32), *([shape((TY, frames, ranks), F32)] * 2)],
        [om_all, *grams],
        [pltpu.VMEM((all_frames, ranks), F32)],
    )
    coef_other = swap(coef_send, group)
    (basis,) = call(basis_kernel, [shape((ranks * share, cols), F32)], [matrix, mix])
    coefficients = jnp.transpose(coef_own + coef_other, (0, 2, 1))[:, None]
    return basis.reshape(ranks, share, cols), coefficients


def solution(mesh):
    in_specs = (P("tm", None, "tile"), P(None, "tile", None, "tm"), P(), P())
    out_specs = (P(None, "tm", "tile"), P(None, "tile", None, "tm"))
    return jax.shard_map(local, mesh=mesh, in_specs=in_specs, out_specs=out_specs, check_vma=False)
```
